256 devices in a mesh: member: 32 (over z, x_hi, core), shard: 8 (over y, x_lo).
Axes of the slice: x: 4 (x_hi: 2, x_lo: 2; x = x_hi * 2 + x_lo), y: 4, z: 8, core: 2. Of those that a mesh axis runs over, the one named last changes fastest.
Arguments:
- tokens: bfloat16 [32, 4096, 4096], P('member', 'shard'), may hold values from -6 to 6
- cotangent: bfloat16 [32, 4096, 1024], P('member', 'shard'), may hold values from -0.59765625 to 0.59765625
- weight: float32 [32, 4096, 1024], P('member', 'shard'), may hold values from -6 to 6
- first_moment: bfloat16 [32, 4096, 1024], P('member', 'shard'), may hold values from -6 to 6
- second_moment: bfloat16 [32, 4096, 1024], P('member', 'shard'), may hold values from 0.5 to 50
- learn_rate: float32 [32], replicated, may hold values from 0.02 to 0.2
- beta_one: float32 [32], replicated, may hold values from 0.8 to 0.95
- beta_two: float32 [32], replicated, may hold values from 0.9 to 0.99
- sources: int32 [32], replicated, may hold values from 0 to 31, as said below
- perturb: int32 [32], replicated, may hold values from 0 to 2
Outputs:
- new_weight: float32 [32, 4096, 1024], P('member', 'shard')
- new_first: bfloat16 [32, 4096, 1024], P('member', 'shard')
- new_second: bfloat16 [32, 4096, 1024], P('member', 'shard')
- new_log_rate: float32 [32], replicated
The draws below stay inside these ranges and needn't reach their ends.
Inputs may be any that keep to these rules, and one draw needn't show every extreme that they name: Exactly 8 members m have sources[m] != m; each of them names one of a set of 8 other members, all of whose entries name themselves. Every other entry equals its index.
All inputs are finite; a program needn't handle non-finite values.
Results may differ from the reference program's by a relative error of at most 0.015.
Values may be sent and summed in bfloat16 or wider, within the bound.
A program may use at most 128 MiB of HBM per device.

```python
import math
import jax
import jax.numpy as jnp
from jax import lax

D = 4096
KVW = 1024
TOKENS = 4096
MEMBERS = 32
STEP = 20


def draw_sources(key, part):
    key = jax.random.fold_in(key, 7)
    order_key, pick_key = jax.random.split(key)
    order = jax.random.permutation(order_key, MEMBERS)
    quarter = MEMBERS // 4
    losers = order[:quarter]
    winners = order[MEMBERS - quarter:]
    picks = jax.random.randint(pick_key, (quarter,), 0, quarter)
    base = jnp.arange(MEMBERS, dtype=jnp.int32)
    return base.at[losers].set(winners[picks].astype(jnp.int32)).astype(jnp.int32)


def with_ends(array, key, smallest, largest):
    index_at = [jax.random.randint(jax.random.fold_in(key, axis), (), 0, length) for axis, length in enumerate(array.shape)]
    main_axis = array.shape.index(max(array.shape))
    neighbour = index_at[:main_axis] + [(index_at[main_axis] + 1) % array.shape[main_axis]] + index_at[main_axis + 1:]
    return array.at[tuple(index_at)].set(smallest).at[tuple(neighbour)].set(largest)


def shard_levels(rng, dims, shards, least, high):
    def one(position, shards_of):
        draws = jax.random.uniform(jax.random.fold_in(jax.random.fold_in(rng, 6), position), (shards_of,), jnp.float32, least / len(shards), high / len(shards))
        return jnp.repeat(jnp.exp(draws), dims[position] // shards_of).reshape((-1,) + (1,) * (len(dims) - position - 1))

    factor_of = one(*shards[0])
    for cut in shards[1:]:
        factor_of = factor_of * one(*cut)
    return factor_of


def bell_draw(stream_key, extent, scale, bound, cuts=(), kind=jnp.bfloat16):
    values = jax.random.normal(stream_key, extent, jnp.float32) * scale
    if len(cuts) > 0:
        values = shard_levels(stream_key, extent, cuts, -0.22, 0.18) * values
    return jnp.clip(values, min=-bound, max=bound).astype(kind)


def setup_inputs(seed: int = 0) -> dict:
    keys = jax.random.split(jax.random.key(seed), 11)
    return {
        "tokens": bell_draw(keys[0], (MEMBERS, TOKENS, D), 1.0, 6.0, ((0, 32), (1, 8))),
        "cotangent": bell_draw(keys[1], (MEMBERS, TOKENS, KVW), 0.1, 0.59765625, ((0, 32), (1, 8))),
        "weight": bell_draw(keys[2], (MEMBERS, D, KVW), 1.0, 6.0, ((0, 32), (1, 8)), jnp.float32),
        "first_moment": bell_draw(keys[3], (MEMBERS, D, KVW), 1.0, 6.0, ((0, 32), (1, 8))),
        "second_moment": jnp.clip(jnp.exp(math.log(50.0) - 4.6051702 * jax.random.uniform(keys[4], (MEMBERS, D, KVW), jnp.float32) ** shard_levels(keys[4], (MEMBERS, D, KVW), ((0, 32), (1, 8)), -0.2, 0.2)), 0.5, 50.0).astype(jnp.bfloat16),
        "learn_rate": jnp.clip(jnp.exp(jax.random.uniform(keys[5], (MEMBERS,), jnp.float32, math.log(0.02), math.log(0.2))), 0.02, 0.2),
        "beta_one": jnp.clip(jax.random.uniform(keys[6], (MEMBERS,), jnp.float32, 0.8, 0.95), 0.8, 0.95),
        "beta_two": jnp.clip(jax.random.uniform(keys[7], (MEMBERS,), jnp.float32, 0.9, 0.99), 0.9, 0.99),
        "sources": draw_sources(jax.random.fold_in(keys[10], 71), 0),
        "perturb": with_ends(jax.random.randint(keys[9], (MEMBERS,), 0, 3), jax.random.fold_in(keys[9], 1), 0, 2).astype(jnp.int32),
    }


def member_step(packed):
    token_rows, cotangent_rows, master, first, second, step_size, decay_one, decay_two = packed
    gradient = jnp.dot(token_rows.T, cotangent_rows, preferred_element_type=jnp.float32)
    moment_one = decay_one * first.astype(jnp.float32) + (1.0 - decay_one) * gradient
    moment_two = decay_two * second.astype(jnp.float32) + (1.0 - decay_two) * gradient * gradient
    corrected_one = moment_one / (1.0 - decay_one ** STEP)
    corrected_two = moment_two / (1.0 - decay_two ** STEP)
    updated = master - step_size * (corrected_one / (jnp.sqrt(corrected_two) + 1e-08) + 0.1 * master)
    return (updated, moment_one.astype(jnp.bfloat16), moment_two.astype(jnp.bfloat16))

def reference(tokens, cotangent, weight, first_moment, second_moment, learn_rate, beta_one, beta_two, sources, perturb):
    updated, first_all, second_all = lax.map(member_step, (tokens, cotangent, weight, first_moment, second_moment, learn_rate, beta_one, beta_two))
    new_weight = jnp.take(updated, sources, axis=0)
    new_first = jnp.take(first_all, sources, axis=0)
    new_second = jnp.take(second_all, sources, axis=0)
    loser = sources != jnp.arange(MEMBERS, dtype=jnp.int32)
    source_rate = jnp.take(learn_rate, sources, axis=0)
    shifted = jnp.log(source_rate) + (perturb - 1).astype(jnp.float32) * math.log(2.0)
    new_log_rate = jnp.where(loser, shifted, jnp.log(learn_rate))
    return (new_weight, new_first, new_second, new_log_rate)
```

```python
import functools
import math

import jax
import jax.numpy as jnp
from jax import lax
from jax.experimental import pallas as pl
from jax.experimental.pallas import tpu as pltpu
from jax.sharding import PartitionSpec as P

MESH = pl.DeviceIdType.MESH
ROWS = 128
SPLIT = 2
LEVELS = 8
QUAD = 4
RING = 4
LAG = {"b": 1, "c": 2, "d": 3, "e": 4, "f": 5, "g": 6, "h": 7}


def twentieth_power(value):
    square = value * value
    fourth = square * square
    eighth = fourth * fourth
    return eighth * eighth * fourth


def step_kernel(
    win_slots,
    lose_slots,
    table,
    rates,
    decays_one,
    decays_two,
    tokens,
    cotangent,
    weight,
    first,
    second,
    out_weight,
    out_first,
    out_second,
    y1_send,
    y1_recv,
    y2_send,
    y2_recv,
    x_send,
    x_recv,
    q1_send,
    q1_recv,
    z1_send,
    z1_recv,
    z2_send,
    z2_recv,
    q2_send,
    q2_recv,
    terms,
    q1_held,
    z1_held,
    z2_held,
    send_sem,
    y1_sem,
    y2_sem,
    x_sem,
    q1_sem,
    z1_sem,
    z2_sem,
    q2_sem,
):
    chunks = y1_send.shape[0]
    cols = y1_send.shape[3]
    part = cols // QUAD
    own_rows = weight.shape[0]
    slots = terms.shape[0]
    member = lax.axis_index("member")
    shard = lax.axis_index("shard")
    level, mine = member // QUAD, lax.rem(member, QUAD)
    y, x_lo = shard // 2, lax.rem(shard, 2)
    y_next, y_prev = lax.rem(y + 1, RING), lax.rem(y + RING - 1, RING)
    y_far = lax.rem(y + 2, RING)

    def on_shard(at_y, at_x):
        return {"member": member, "shard": at_y * 2 + at_x}

    def on_member(at_level, at_quad):
        return {"member": at_level * QUAD + at_quad, "shard": shard}

    up, down = on_shard(y_next, x_lo), on_shard(y_prev, x_lo)
    beside = on_shard(y, 1 - x_lo)
    quads = [lax.rem(mine + d, QUAD) for d in range(1, QUAD)]
    levels = [lax.rem(level + d, LEVELS) for d in (4, 3, 5, 2, 6, 1, 7)]

    peers = [up, down, beside]
    peers += [on_member(level, q) for q in quads]
    peers += [on_member(z, mine) for z in levels]
    barrier = pltpu.get_barrier_semaphore()
    for peer in peers:
        pl.semaphore_signal(barrier, inc=1, device_id=peer, device_id_type=MESH)
    pl.semaphore_wait(barrier, len(peers))

    def send(src, dst, stage, recv, device):
        pltpu.make_async_remote_copy(
            src_ref=src,
            dst_ref=dst,
            send_sem=send_sem.at[stage],
            recv_sem=recv,
            device_id=device,
            device_id_type=MESH,
        ).start()

    def await_bytes(ref, sem):
        pltpu.make_async_copy(ref, ref, sem).wait()

    def place(k):
        row = pl.multiple_of((k // SPLIT) * ROWS, ROWS)
        col = pl.multiple_of(lax.rem(k, SPLIT) * cols, cols)
        return row, col

    def term(k, at_y, at_x):
        row, col = place(k)
        start = pl.multiple_of((at_y * 2 + at_x) * own_rows + row, ROWS)
        return lax.dot_general(
            tokens[:, pl.ds(start, ROWS)],
            cotangent[:, pl.ds(col, cols)],
            (((0,), (0,)), ((), ())),
            preferred_element_type=jnp.float32,
        )

    def stage_a(k):
        slot = lax.rem(k, slots)
        y1_send[k, 0] = term(k, y_far, 0).astype(jnp.bfloat16)
        send(y1_send.at[k, 0], y1_recv.at[k, 0], 0, y1_sem.at[k, 0], up)
        y1_send[k, 1] = term(k, y_far, 1).astype(jnp.bfloat16)
        send(y1_send.at[k, 1], y1_recv.at[k, 1], 0, y1_sem.at[k, 1], down)
        y2_send[k, 0, 1] = term(k, y_next, 1).astype(jnp.bfloat16)
        send(y2_send.at[k, 0, 1], y2_recv.at[k, 0, 1], 1, y2_sem.at[k, 0], up)
        y2_send[k, 1, 0] = term(k, y_prev, 0).astype(jnp.bfloat16)
        send(y2_send.at[k, 1, 0], y2_recv.at[k, 1, 0], 1, y2_sem.at[k, 1], down)
        terms[slot, 0] = term(k, y_next, 0)
        terms[slot, 1] = term(k, y_prev, 1)
        terms[slot, 2] = term(k, y, 1 - x_lo)
        terms[slot, 3] = term(k, y, x_lo)

    def stage_b(k):
        slot = lax.rem(k, slots)
        await_bytes(y1_recv.at[k, 0], y1_sem.at[k, 0])
        y2_send[k, 0, 0] = (terms[slot, 0] + y1_recv[k, 0].astype(jnp.float32)).astype(jnp.bfloat16)
        send(y2_send.at[k, 0, 0], y2_recv.at[k, 0, 0], 1, y2_sem.at[k, 0], up)
        await_bytes(y1_recv.at[k, 1], y1_sem.at[k, 1])
        y2_send[k, 1, 1] = (terms[slot, 1] + y1_recv[k, 1].astype(jnp.float32)).astype(jnp.bfloat16)
        send(y2_send.at[k, 1, 1], y2_recv.at[k, 1, 1], 1, y2_sem.at[k, 1], down)

    def stage_c(k):
        slot = lax.rem(k, slots)
        await_bytes(y2_recv.at[k, 0], y2_sem.at[k, 0])
        await_bytes(y2_recv.at[k, 1], y2_sem.at[k, 1])

        def total(which, at_x):
            return (
                terms[slot, which]
                + y2_recv[k, 0, at_x].astype(jnp.float32)
                + y2_recv[k, 1, at_x].astype(jnp.float32)
            )

        x_send[k] = total(2, 1 - x_lo).astype(jnp.bfloat16)
        send(x_send.at[k], x_recv.at[k], 2, x_sem.at[k], beside)
        terms[slot, 3] = total(3, x_lo)

    def stage_d(k):
        slot = lax.rem(k, slots)
        row, col = place(k)
        here = (pl.ds(row, ROWS), pl.ds(col, cols))
        rate = jnp.full((1, cols), rates[member], jnp.float32)
        decay_one = jnp.full((1, cols), decays_one[member], jnp.float32)
        decay_two = jnp.full((1, cols), decays_two[member], jnp.float32)
        scale_one = 1.0 / (1.0 - twentieth_power(decay_one))
        scale_two = 1.0 / (1.0 - twentieth_power(decay_two))
        await_bytes(x_recv.at[k], x_sem.at[k])
        gradient = terms[slot, 3] + x_recv[k].astype(jnp.float32)
        moment_one = decay_one * first[here].astype(jnp.float32) + (1.0 - decay_one) * gradient
        moment_two = (
            decay_two * second[here].astype(jnp.float32) + (1.0 - decay_two) * gradient * gradient
        )
        master = weight[here]
        updated = master - rate * (
            (moment_one * scale_one) / (jnp.sqrt(moment_two * scale_two) + 1e-08) + 0.1 * master
        )
        out_weight[here] = updated
        narrow = (
            updated.astype(jnp.bfloat16),
            moment_one.astype(jnp.bfloat16),
            moment_two.astype(jnp.bfloat16),
        )
        out_first[here] = narrow[1]
        out_second[here] = narrow[2]
        for q in range(QUAD):
            for a in range(3):
                q1_send[k, q, a] = narrow[a][:, q * part : (q + 1) * part]
        for q in quads:
            send(q1_send.at[k, q], q1_recv.at[k, mine], 3, q1_sem.at[k], on_member(level, q))
        q1_recv[k, mine] = q1_send[k, mine]

    def stage_e(k):
        await_bytes(q1_recv.at[k, pl.ds(0, QUAD - 1)], q1_sem.at[k])
        q1_held[...] = q1_recv[k]
        for j in range(win_slots):
            chosen = q1_held[table[level * QUAD + j]]
            for z in range(LEVELS):
                z1_send[k, z, j] = chosen[:, z * 16 : (z + 1) * 16, :]
        for z in levels:
            send(z1_send.at[k, z], z1_recv.at[k, level], 4, z1_sem.at[k], on_member(z, mine))
        z1_recv[k, level] = z1_send[k, level]

    def stage_f(k):
        await_bytes(z1_recv.at[k, pl.ds(0, LEVELS - 1)], z1_sem.at[k])
        z1_held[...] = z1_recv[k]
        for z in range(LEVELS):
            for j in range(lose_slots):
                source = table[32 + z * QUAD + j]
                z2_send[k, z, j] = z1_held[source // QUAD, lax.rem(source, QUAD)]
        for z in levels:
            send(z2_send.at[k, z], z2_recv.at[k, level], 5, z2_sem.at[k], on_member(z, mine))
        z2_recv[k, level] = z2_send[k, level]

    def stage_g(k):
        await_bytes(z2_recv.at[k, pl.ds(0, LEVELS - 1)], z2_sem.at[k])
        z2_held[...] = z2_recv[k]
        for q in range(QUAD):
            slot = table[64 + level * QUAD + q]
            for z in range(LEVELS):
                q2_send[k, q, z] = z2_held[z, slot]
        for q in quads:
            send(q2_send.at[k, q], q2_recv.at[k, mine], 6, q2_sem.at[k], on_member(level, q))
        q2_recv[k, mine] = q2_send[k, mine]

    def stage_h(k):
        row, col = place(k)
        await_bytes(q2_recv.at[k, pl.ds(0, QUAD - 1)], q2_sem.at[k])
        taken = jnp.full((1, part), table[96 + member], jnp.int32) != 0
        outs = (out_weight, out_first, out_second)
        for q in range(QUAD):
            for a in range(3):
                here = (pl.ds(row, ROWS), pl.ds(col + q * part, part))
                copied = q2_recv[k, q, :, a].reshape(ROWS, part).astype(jnp.float32)
                kept = outs[a][here].astype(jnp.float32)
                outs[a][here] = jnp.where(taken, copied, kept).astype(outs[a].dtype)

    stages = (
        (0, stage_a),
        (LAG["b"], stage_b),
        (LAG["c"], stage_c),
        (LAG["d"], stage_d),
        (LAG["e"], stage_e),
        (LAG["f"], stage_f),
        (LAG["g"], stage_g),
        (LAG["h"], stage_h),
    )

    def iteration(i, carry):
        for lag, stage in stages:
            k = i - lag

            @pl.when((k >= 0) & (k < chunks))
            def _():
                stage(k)

        return carry

    lax.fori_loop(0, chunks + LAG["h"], iteration, 0)

    sent = (
        y1_send,
        y2_send,
        x_send,
        q1_send.at[:, pl.ds(0, QUAD - 1)],
        z1_send.at[:, pl.ds(0, LEVELS - 1)],
        z2_send.at[:, pl.ds(0, LEVELS - 1)],
        q2_send.at[:, pl.ds(0, QUAD - 1)],
    )
    for stage, ref in enumerate(sent):
        await_bytes(ref, send_sem.at[stage])


def step_call(win_slots, lose_slots, collective_id, table, rates, ones, twos, *blocks):
    tokens, cotangent, weight, first, second = blocks
    rows, width = weight.shape
    cols = width // SPLIT
    chunks = rows // ROWS * SPLIT
    part = cols // QUAD
    kind = jnp.bfloat16
    scalars = pl.BlockSpec(memory_space=pltpu.SMEM)
    whole = pl.BlockSpec(memory_space=pltpu.VMEM)
    y1 = pltpu.VMEM((chunks, 2, ROWS, cols), kind)
    y2 = pltpu.VMEM((chunks, 2, 2, ROWS, cols), kind)
    beside = pltpu.VMEM((chunks, ROWS, cols), kind)
    q1 = pltpu.VMEM((chunks, QUAD, 3, ROWS, part), kind)
    z1 = pltpu.VMEM((chunks, LEVELS, win_slots, 3, ROWS // LEVELS, part), kind)
    z2 = pltpu.VMEM((chunks, LEVELS, lose_slots, 3, ROWS // LEVELS, part), kind)
    q2 = pltpu.VMEM((chunks, QUAD, LEVELS, 3, ROWS // LEVELS, part), kind)
    dma = pltpu.SemaphoreType.DMA
    return pl.pallas_call(
        functools.partial(step_kernel, win_slots, lose_slots),
        out_shape=(
            jax.ShapeDtypeStruct(weight.shape, jnp.float32),
            jax.ShapeDtypeStruct(weight.shape, kind),
            jax.ShapeDtypeStruct(weight.shape, kind),
        ),
        in_specs=[scalars] * 4 + [whole] * 5,
        out_specs=(whole, whole, whole),
        scratch_shapes=[
            y1,
            y1,
            y2,
            y2,
            beside,
            beside,
            q1,
            q1,
            z1,
            z1,
            z2,
            z2,
            q2,
            q2,
            pltpu.VMEM((LAG["d"] + 1, 4, ROWS, cols), jnp.float32),
            pltpu.VMEM(q1.shape[1:], kind),
            pltpu.VMEM(z1.shape[1:], kind),
            pltpu.VMEM(z2.shape[1:], kind),
            dma((7,)),
            dma((chunks, 2)),
            dma((chunks, 2)),
            dma((chunks,)),
            dma((chunks,)),
            dma((chunks,)),
            dma((chunks,)),
            dma((chunks,)),
        ],
        compiler_params=pltpu.CompilerParams(
            collective_id=collective_id,
            has_side_effects=True,
            vmem_limit_bytes=63 * 2**20,
        ),
    )(table, rates, ones, twos, *blocks)


def routes(sources):
    members = sources.shape[0]
    own = jnp.arange(members, dtype=jnp.int32)
    loser = sources != own
    equal = sources[:, None] == own[None, :]
    winner = jnp.any(equal & loser[:, None], axis=0)

    def ranks(flags):
        flat = flags.reshape(LEVELS, QUAD).astype(jnp.int32)
        before = jnp.tril(jnp.ones((QUAD, QUAD), jnp.int32), -1)
        rank = jnp.sum(flat[:, None, :] * before[None], axis=2)
        return flat, rank

    win, win_rank = ranks(winner)
    lose, lose_rank = ranks(loser)
    column = jnp.arange(QUAD, dtype=jnp.int32)

    def spread(flat, rank, value):
        at = (rank[:, :, None] == column[None, None, :]) & (flat[:, :, None] != 0)
        return jnp.sum(jnp.where(at, value[:, :, None], 0), axis=1)

    chosen = spread(win, win_rank, jnp.broadcast_to(column[None, :], win.shape))
    place = (own // QUAD) * QUAD + win_rank.reshape(members)
    source_place = jnp.sum(jnp.where(equal, place[None, :], 0), axis=1)
    wanted = spread(lose, lose_rank, source_place.reshape(LEVELS, QUAD))
    slot = jnp.where(lose != 0, lose_rank, 0)
    table = jnp.concatenate(
        [chosen.reshape(-1), wanted.reshape(-1), slot.reshape(-1), loser.astype(jnp.int32)]
    )
    return table, loser, equal


def on_device(
    tokens,
    cotangent,
    weight,
    first_moment,
    second_moment,
    learn_rate,
    beta_one,
    beta_two,
    sources,
    perturb,
):
    table, loser, equal = routes(sources)
    new_weight, new_first, new_second = step_call(
        QUAD,
        QUAD,
        0,
        table,
        learn_rate,
        beta_one,
        beta_two,
        tokens[0],
        cotangent[0],
        weight[0],
        first_moment[0],
        second_moment[0],
    )
    source_rate = jnp.sum(jnp.where(equal, learn_rate[None, :], 0.0), axis=1)
    shifted = jnp.log(source_rate) + (perturb - 1).astype(jnp.float32) * math.log(2.0)
    new_log_rate = jnp.where(loser, shifted, jnp.log(learn_rate))
    return new_weight[None], new_first[None], new_second[None], new_log_rate


def solution(mesh):
    block = P("member", "shard", None)
    return jax.shard_map(
        on_device,
        mesh=mesh,
        in_specs=(block,) * 5 + (P(),) * 5,
        out_specs=(block, block, block, P()),
        check_vma=False,
    )
```

```python
import functools
import math

import jax
import jax.numpy as jnp
from jax import lax
from jax.experimental import pallas as pl
from jax.experimental.pallas import tpu as pltpu
from jax.sharding import PartitionSpec as P

MESH = pl.DeviceIdType.MESH
ROWS = 128
SPLIT = 2
LEVELS = 8
QUAD = 4
RING = 4
PLANS = (
    (2, "edgbafhc", dict(a=0, b=1, c=1, d=3, e=4, f=5, g=8, h=9)),
    (3, "acgbefdh", dict(a=0, b=0, c=1, d=1, e=2, f=3, g=5, h=6)),
    (4, "acbeghfd", dict(a=0, b=0, c=1, d=1, e=2, f=3, g=7, h=9)),
)


def twentieth_power(value):
    square = value * value
    fourth = square * square
    eighth = fourth * fourth
    return eighth * eighth * fourth


def step_kernel(
    member_slots,
    order,
    lags,
    table,
    rates,
    decays_one,
    decays_two,
    tokens,
    cotangent,
    weight,
    first,
    second,
    out_weight,
    out_first,
    out_second,
    y1_send,
    y1_recv,
    y2_send,
    y2_recv,
    x_send,
    x_recv,
    q1_send,
    q1_recv,
    z1_send,
    z1_recv,
    z2_send,
    z2_recv,
    q2_send,
    q2_recv,
    terms,
    q1_held,
    z1_held,
    z2_held,
    send_sem,
    y1_sem,
    y2_sem,
    x_sem,
    q1_sem,
    z1_sem,
    z2_sem,
    q2_sem,
):
    chunks = y1_send.shape[0]
    cols = y1_send.shape[3]
    part = cols // QUAD
    own_rows = weight.shape[0]
    slots = terms.shape[0]
    member = lax.axis_index("member")
    shard = lax.axis_index("shard")
    level, mine = member // QUAD, lax.rem(member, QUAD)
    y, x_lo = shard // 2, lax.rem(shard, 2)
    y_next, y_prev = lax.rem(y + 1, RING), lax.rem(y + RING - 1, RING)
    y_far = lax.rem(y + 2, RING)

    def on_shard(at_y, at_x):
        return {"member": member, "shard": at_y * 2 + at_x}

    def on_member(at_level, at_quad):
        return {"member": at_level * QUAD + at_quad, "shard": shard}

    up, down = on_shard(y_next, x_lo), on_shard(y_prev, x_lo)
    beside = on_shard(y, 1 - x_lo)
    quads = [lax.rem(mine + d, QUAD) for d in range(1, QUAD)]
    levels = [lax.rem(level + d, LEVELS) for d in (4, 3, 5, 2, 6, 1, 7)]

    peers = [up, down, beside]
    peers += [on_member(level, q) for q in quads]
    peers += [on_member(z, mine) for z in levels]
    barrier = pltpu.get_barrier_semaphore()
    for peer in peers:
        pl.semaphore_signal(barrier, inc=1, device_id=peer, device_id_type=MESH)
    pl.semaphore_wait(barrier, len(peers))

    def send(src, dst, stage, recv, device):
        pltpu.make_async_remote_copy(
            src_ref=src,
            dst_ref=dst,
            send_sem=send_sem.at[stage],
            recv_sem=recv,
            device_id=device,
            device_id_type=MESH,
        ).start()

    def await_bytes(ref, sem):
        pltpu.make_async_copy(ref, ref, sem).wait()

    def place(k):
        row = pl.multiple_of((k // SPLIT) * ROWS, ROWS)
        col = pl.multiple_of(lax.rem(k, SPLIT) * cols, cols)
        return row, col

    def term(k, at_y, at_x):
        row, col = place(k)
        start = pl.multiple_of((at_y * 2 + at_x) * own_rows + row, ROWS)
        return lax.dot_general(
            tokens[:, pl.ds(start, ROWS)],
            cotangent[:, pl.ds(col, cols)],
            (((0,), (0,)), ((), ())),
            preferred_element_type=jnp.float32,
        )

    def stage_a(k):
        slot = lax.rem(k, slots)
        y1_send[k, 0] = term(k, y_far, 0).astype(jnp.bfloat16)
        send(y1_send.at[k, 0], y1_recv.at[k, 0], 0, y1_sem.at[k, 0], up)
        y1_send[k, 1] = term(k, y_far, 1).astype(jnp.bfloat16)
        send(y1_send.at[k, 1], y1_recv.at[k, 1], 0, y1_sem.at[k, 1], down)
        y2_send[k, 0, 1] = term(k, y_next, 1).astype(jnp.bfloat16)
        send(y2_send.at[k, 0, 1], y2_recv.at[k, 0, 1], 1, y2_sem.at[k, 0], up)
        y2_send[k, 1, 0] = term(k, y_prev, 0).astype(jnp.bfloat16)
        send(y2_send.at[k, 1, 0], y2_recv.at[k, 1, 0], 1, y2_sem.at[k, 1], down)
        terms[slot, 0] = term(k, y_next, 0)
        terms[slot, 1] = term(k, y_prev, 1)
        terms[slot, 2] = term(k, y, 1 - x_lo)
        terms[slot, 3] = term(k, y, x_lo)

    def stage_b(k):
        slot = lax.rem(k, slots)
        await_bytes(y1_recv.at[k, 0], y1_sem.at[k, 0])
        y2_send[k, 0, 0] = (terms[slot, 0] + y1_recv[k, 0].astype(jnp.float32)).astype(jnp.bfloat16)
        send(y2_send.at[k, 0, 0], y2_recv.at[k, 0, 0], 1, y2_sem.at[k, 0], up)
        await_bytes(y1_recv.at[k, 1], y1_sem.at[k, 1])
        y2_send[k, 1, 1] = (terms[slot, 1] + y1_recv[k, 1].astype(jnp.float32)).astype(jnp.bfloat16)
        send(y2_send.at[k, 1, 1], y2_recv.at[k, 1, 1], 1, y2_sem.at[k, 1], down)

    def stage_c(k):
        slot = lax.rem(k, slots)
        await_bytes(y2_recv.at[k, 0], y2_sem.at[k, 0])
        await_bytes(y2_recv.at[k, 1], y2_sem.at[k, 1])

        def total(which, at_x):
            return (
                terms[slot, which]
                + y2_recv[k, 0, at_x].astype(jnp.float32)
                + y2_recv[k, 1, at_x].astype(jnp.float32)
            )

        x_send[k] = total(2, 1 - x_lo).astype(jnp.bfloat16)
        send(x_send.at[k], x_recv.at[k], 2, x_sem.at[k], beside)
        terms[slot, 3] = total(3, x_lo)

    def stage_d(k):
        slot = lax.rem(k, slots)
        row, col = place(k)
        here = (pl.ds(row, ROWS), pl.ds(col, cols))
        rate = jnp.full((1, cols), rates[member], jnp.float32)
        decay_one = jnp.full((1, cols), decays_one[member], jnp.float32)
        decay_two = jnp.full((1, cols), decays_two[member], jnp.float32)
        scale_one = 1.0 / (1.0 - twentieth_power(decay_one))
        scale_two = 1.0 / (1.0 - twentieth_power(decay_two))
        await_bytes(x_recv.at[k], x_sem.at[k])
        gradient = terms[slot, 3] + x_recv[k].astype(jnp.float32)
        moment_one = decay_one * first[here].astype(jnp.float32) + (1.0 - decay_one) * gradient
        moment_two = (
            decay_two * second[here].astype(jnp.float32) + (1.0 - decay_two) * gradient * gradient
        )
        master = weight[here]
        updated = master - rate * (
            (moment_one * scale_one) / (jnp.sqrt(moment_two * scale_two) + 1e-08) + 0.1 * master
        )
        out_weight[here] = updated
        narrow = (
            updated.astype(jnp.bfloat16),
            moment_one.astype(jnp.bfloat16),
            moment_two.astype(jnp.bfloat16),
        )
        out_first[here] = narrow[1]
        out_second[here] = narrow[2]
        for q in range(QUAD):
            for a in range(3):
                q1_send[k, q, a] = narrow[a][:, q * part : (q + 1) * part]
        for q in quads:
            send(q1_send.at[k, q], q1_recv.at[k, mine], 3, q1_sem.at[k], on_member(level, q))
        q1_recv[k, mine] = q1_send[k, mine]

    def stage_e(k):
        await_bytes(q1_recv.at[k, pl.ds(0, QUAD - 1)], q1_sem.at[k])
        q1_held[...] = q1_recv[k]
        for j in range(member_slots):
            chosen = q1_held[table[level * QUAD + j]]
            for z in range(LEVELS):
                z1_send[k, z, j] = chosen[:, z * 16 : (z + 1) * 16, :]
        for z in levels:
            send(z1_send.at[k, z], z1_recv.at[k, level], 4, z1_sem.at[k], on_member(z, mine))
        z1_recv[k, level] = z1_send[k, level]

    def stage_f(k):
        await_bytes(z1_recv.at[k, pl.ds(0, LEVELS - 1)], z1_sem.at[k])
        z1_held[...] = z1_recv[k]
        for z in range(LEVELS):
            for j in range(member_slots):
                source = table[32 + z * QUAD + j]
                z2_send[k, z, j] = z1_held[source // QUAD, lax.rem(source, QUAD)]
        for z in levels:
            send(z2_send.at[k, z], z2_recv.at[k, level], 5, z2_sem.at[k], on_member(z, mine))
        z2_recv[k, level] = z2_send[k, level]

    def stage_g(k):
        await_bytes(z2_recv.at[k, pl.ds(0, LEVELS - 1)], z2_sem.at[k])
        z2_held[...] = z2_recv[k]
        for q in range(QUAD):
            slot = table[64 + level * QUAD + q]
            for z in range(LEVELS):
                q2_send[k, q, z] = z2_held[z, slot]
        for q in quads:
            send(q2_send.at[k, q], q2_recv.at[k, mine], 6, q2_sem.at[k], on_member(level, q))
        q2_recv[k, mine] = q2_send[k, mine]

    def stage_h(k):
        row, col = place(k)
        await_bytes(q2_recv.at[k, pl.ds(0, QUAD - 1)], q2_sem.at[k])
        taken = jnp.full((1, part), table[96 + member], jnp.int32) != 0
        outs = (out_weight, out_first, out_second)
        for q in range(QUAD):
            for a in range(3):
                here = (pl.ds(row, ROWS), pl.ds(col + q * part, part))
                copied = q2_recv[k, q, :, a].reshape(ROWS, part).astype(jnp.float32)
                kept = outs[a][here].astype(jnp.float32)
                outs[a][here] = jnp.where(taken, copied, kept).astype(outs[a].dtype)

    stages = dict(
        a=stage_a,
        b=stage_b,
        c=stage_c,
        d=stage_d,
        e=stage_e,
        f=stage_f,
        g=stage_g,
        h=stage_h,
    )

    def iteration(i, carry):
        for name in order:
            k = i - lags[name]

            @pl.when((k >= 0) & (k < chunks))
            def _():
                stages[name](k)

        return carry

    lax.fori_loop(0, chunks + lags["h"], iteration, 0)

    sent = (
        y1_send,
        y2_send,
        x_send,
        q1_send.at[:, pl.ds(0, QUAD - 1)],
        z1_send.at[:, pl.ds(0, LEVELS - 1)],
        z2_send.at[:, pl.ds(0, LEVELS - 1)],
        q2_send.at[:, pl.ds(0, QUAD - 1)],
    )
    for stage, ref in enumerate(sent):
        await_bytes(ref, send_sem.at[stage])


def step_call(plan, table, rates, ones, twos, *blocks):
    member_slots, order, lags = PLANS[plan]
    tokens, cotangent, weight, first, second = blocks
    rows, width = weight.shape
    cols = width // SPLIT
    chunks = rows // ROWS * SPLIT
    part = cols // QUAD
    kind = jnp.bfloat16
    scalars = pl.BlockSpec(memory_space=pltpu.SMEM)
    whole = pl.BlockSpec(memory_space=pltpu.VMEM)
    y1 = pltpu.VMEM((chunks, 2, ROWS, cols), kind)
    y2 = pltpu.VMEM((chunks, 2, 2, ROWS, cols), kind)
    beside = pltpu.VMEM((chunks, ROWS, cols), kind)
    q1 = pltpu.VMEM((chunks, QUAD, 3, ROWS, part), kind)
    z1 = pltpu.VMEM((chunks, LEVELS, member_slots, 3, ROWS // LEVELS, part), kind)
    z2 = pltpu.VMEM((chunks, LEVELS, member_slots, 3, ROWS // LEVELS, part), kind)
    q2 = pltpu.VMEM((chunks, QUAD, LEVELS, 3, ROWS // LEVELS, part), kind)
    dma = pltpu.SemaphoreType.DMA
    return pl.pallas_call(
        functools.partial(step_kernel, member_slots, order, lags),
        out_shape=(
            jax.ShapeDtypeStruct(weight.shape, jnp.float32),
            jax.ShapeDtypeStruct(weight.shape, kind),
            jax.ShapeDtypeStruct(weight.shape, kind),
        ),
        in_specs=[scalars] * 4 + [whole] * 5,
        out_specs=(whole, whole, whole),
        scratch_shapes=[
            y1,
            y1,
            y2,
            y2,
            beside,
            beside,
            q1,
            q1,
            z1,
            z1,
            z2,
            z2,
            q2,
            q2,
            pltpu.VMEM((lags["d"] + 1, 4, ROWS, cols), jnp.float32),
            pltpu.VMEM(q1.shape[1:], kind),
            pltpu.VMEM(z1.shape[1:], kind),
            pltpu.VMEM(z2.shape[1:], kind),
            dma((7,)),
            dma((chunks, 2)),
            dma((chunks, 2)),
            dma((chunks,)),
            dma((chunks,)),
            dma((chunks,)),
            dma((chunks,)),
            dma((chunks,)),
        ],
        compiler_params=pltpu.CompilerParams(
            collective_id=plan,
            has_side_effects=True,
            vmem_limit_bytes=63 * 2**20,
        ),
    )(table, rates, ones, twos, *blocks)


def routes(sources):
    members = sources.shape[0]
    own = jnp.arange(members, dtype=jnp.int32)
    loser = sources != own
    equal = sources[:, None] == own[None, :]
    winner = jnp.any(equal & loser[:, None], axis=0)

    def ranks(flags):
        flat = flags.reshape(LEVELS, QUAD).astype(jnp.int32)
        before = jnp.tril(jnp.ones((QUAD, QUAD), jnp.int32), -1)
        rank = jnp.sum(flat[:, None, :] * before[None], axis=2)
        return flat, rank

    win, win_rank = ranks(winner)
    lose, lose_rank = ranks(loser)
    column = jnp.arange(QUAD, dtype=jnp.int32)

    def spread(flat, rank, value):
        at = (rank[:, :, None] == column[None, None, :]) & (flat[:, :, None] != 0)
        return jnp.sum(jnp.where(at, value[:, :, None], 0), axis=1)

    chosen = spread(win, win_rank, jnp.broadcast_to(column[None, :], win.shape))
    place = (own // QUAD) * QUAD + win_rank.reshape(members)
    source_place = jnp.sum(jnp.where(equal, place[None, :], 0), axis=1)
    wanted = spread(lose, lose_rank, source_place.reshape(LEVELS, QUAD))
    slot = jnp.where(lose != 0, lose_rank, 0)
    table = jnp.concatenate(
        [chosen.reshape(-1), wanted.reshape(-1), slot.reshape(-1), loser.astype(jnp.int32)]
    )
    most = jnp.max(jnp.maximum(jnp.sum(win, axis=1), jnp.sum(lose, axis=1)))
    return table, most, loser, equal


def on_device(
    tokens,
    cotangent,
    weight,
    first_moment,
    second_moment,
    learn_rate,
    beta_one,
    beta_two,
    sources,
    perturb,
):
    table, most, loser, equal = routes(sources)
    plan = jnp.clip(most - PLANS[0][0], 0, len(PLANS) - 1)
    new_weight, new_first, new_second = lax.switch(
        plan,
        [functools.partial(step_call, which) for which in range(len(PLANS))],
        table,
        learn_rate,
        beta_one,
        beta_two,
        tokens[0],
        cotangent[0],
        weight[0],
        first_moment[0],
        second_moment[0],
    )
    source_rate = jnp.sum(jnp.where(equal, learn_rate[None, :], 0.0), axis=1)
    shifted = jnp.log(source_rate) + (perturb - 1).astype(jnp.float32) * math.log(2.0)
    new_log_rate = jnp.where(loser, shifted, jnp.log(learn_rate))
    return new_weight[None], new_first[None], new_second[None], new_log_rate


def solution(mesh):
    block = P("member", "shard", None)
    return jax.shard_map(
        on_device,
        mesh=mesh,
        in_specs=(block,) * 5 + (P(),) * 5,
        out_specs=(block, block, block, P()),
        check_vma=False,
    )
```

```python
import functools
import math

import jax
import jax.numpy as jnp
from jax import lax
from jax.experimental import pallas as pl
from jax.experimental.pallas import tpu as pltpu
from jax.sharding import PartitionSpec as P

MESH = pl.DeviceIdType.MESH
ROWS = 128
SPLIT = 2
LEVELS = 8
QUAD = 4
RING = 4
EARLY = 4
PLANS = (
    (2, 2, "fchrdgbeap", dict(a=0, b=1, c=2, d=3, e=4, f=6, g=7, h=9, p=0, r=2)),
    (2, 3, "redchpbfga", dict(a=0, b=1, c=2, d=3, e=4, f=5, g=7, h=9, p=0, r=2)),
    (3, 3, "gphredcbaf", dict(a=0, b=1, c=2, d=3, e=4, f=5, g=8, h=10, p=0, r=1)),
    (4, 4, "rbpedfaghc", dict(a=0, b=1, c=2, d=3, e=4, f=7, g=9, h=9, p=0, r=1)),
)


def twentieth_power(value):
    square = value * value
    fourth = square * square
    eighth = fourth * fourth
    return eighth * eighth * fourth


def adam(master, first, second, gradient, rate, decay_one, decay_two):
    scale_one = 1.0 / (1.0 - twentieth_power(decay_one))
    scale_two = 1.0 / (1.0 - twentieth_power(decay_two))
    moment_one = decay_one * first + (1.0 - decay_one) * gradient
    moment_two = decay_two * second + (1.0 - decay_two) * gradient * gradient
    updated = master - rate * (
        (moment_one * scale_one) / (jnp.sqrt(moment_two * scale_two) + 1e-08) + 0.1 * master
    )
    return updated, moment_one, moment_two


def step_kernel(
    win_slots,
    lose_slots,
    order,
    lags,
    table,
    rates,
    decays_one,
    decays_two,
    tokens_in,
    cotangent_in,
    weight_in,
    first_in,
    second_in,
    weight_out,
    first_out,
    second_out,
    tokens,
    cotangent,
    weight,
    first,
    second,
    out_weight,
    out_first,
    out_second,
    y1_send,
    y1_recv,
    y2_send,
    y2_recv,
    x_send,
    x_recv,
    q1_send,
    q1_recv,
    z1_send,
    z1_recv,
    z2_send,
    z2_recv,
    q2_send,
    q2_recv,
    g1_send,
    g1_recv,
    g2_send,
    g2_recv,
    terms,
    q1_held,
    z1_held,
    z2_held,
    g1_held,
    load_sem,
    out_sem,
    send_sem,
    y1_sem,
    y2_sem,
    x_sem,
    q1_sem,
    z1_sem,
    z2_sem,
    q2_sem,
    g1_sem,
    g2_sem,
):
    chunks = y1_send.shape[0]
    cols = y1_send.shape[3]
    plain = chunks - EARLY
    part = cols // QUAD
    own_rows = weight.shape[0]
    slots = terms.shape[0]
    member = lax.axis_index("member")
    shard = lax.axis_index("shard")
    level, mine = member // QUAD, lax.rem(member, QUAD)
    y, x_lo = shard // 2, lax.rem(shard, 2)
    y_next, y_prev = lax.rem(y + 1, RING), lax.rem(y + RING - 1, RING)
    y_far = lax.rem(y + 2, RING)

    def on_shard(at_y, at_x):
        return {"member": member, "shard": at_y * 2 + at_x}

    def on_member(at_level, at_quad):
        return {"member": at_level * QUAD + at_quad, "shard": shard}

    up, down = on_shard(y_next, x_lo), on_shard(y_prev, x_lo)
    beside = on_shard(y, 1 - x_lo)
    quads = [lax.rem(mine + d, QUAD) for d in range(1, QUAD)]
    levels = [lax.rem(level + d, LEVELS) for d in (4, 3, 5, 2, 6, 1, 7)]

    row_parts = own_rows // ROWS
    blocks = tokens.shape[1] // own_rows

    def load(src, dst, which):
        pltpu.make_async_copy(src, dst, load_sem.at[which]).start()

    def load_tokens(part_of_rows):
        for b in range(blocks):
            here = pl.ds(b * own_rows + part_of_rows * ROWS, ROWS)
            load(tokens_in.at[:, here], tokens.at[:, here], part_of_rows)

    load(cotangent_in, cotangent, row_parts)
    load_tokens(0)
    load(weight_in, weight, row_parts + 1)
    load(first_in, first, row_parts + 2)
    load(second_in, second, row_parts + 3)
    for r in range(1, row_parts):
        load_tokens(r)

    peers = [up, down, beside]
    peers += [on_member(level, q) for q in quads]
    peers += [on_member(z, mine) for z in levels]
    barrier = pltpu.get_barrier_semaphore()
    for peer in peers:
        pl.semaphore_signal(barrier, inc=1, device_id=peer, device_id_type=MESH)
    pl.semaphore_wait(barrier, len(peers))

    def send(src, dst, stage, recv, device):
        pltpu.make_async_remote_copy(
            src_ref=src,
            dst_ref=dst,
            send_sem=send_sem.at[stage],
            recv_sem=recv,
            device_id=device,
            device_id_type=MESH,
        ).start()

    def await_bytes(ref, sem):
        pltpu.make_async_copy(ref, ref, sem).wait()

    def place(k):
        row = pl.multiple_of((k // SPLIT) * ROWS, ROWS)
        col = pl.multiple_of(lax.rem(k, SPLIT) * cols, cols)
        return row, col

    def term(k, at_y, at_x):
        row, col = place(k)
        start = pl.multiple_of((at_y * 2 + at_x) * own_rows + row, ROWS)
        return lax.dot_general(
            tokens[:, pl.ds(start, ROWS)],
            cotangent[:, pl.ds(col, cols)],
            (((0,), (0,)), ((), ())),
            preferred_element_type=jnp.float32,
        )

    def stage_a(k):
        slot = lax.rem(k, slots)

        @pl.when(k == 0)
        def _():
            await_bytes(cotangent, load_sem.at[row_parts])

        @pl.when(lax.rem(k, SPLIT) == 0)
        def _():
            await_bytes(tokens.at[:, pl.ds(0, blocks * ROWS)], load_sem.at[k // SPLIT])

        y1_send[k, 0] = term(k, y_far, 0).astype(jnp.bfloat16)
        send(y1_send.at[k, 0], y1_recv.at[k, 0], 0, y1_sem.at[k, 0], up)
        y1_send[k, 1] = term(k, y_far, 1).astype(jnp.bfloat16)
        send(y1_send.at[k, 1], y1_recv.at[k, 1], 0, y1_sem.at[k, 1], down)
        y2_send[k, 0, 1] = term(k, y_next, 1).astype(jnp.bfloat16)
        send(y2_send.at[k, 0, 1], y2_recv.at[k, 0, 1], 1, y2_sem.at[k, 0], up)
        y2_send[k, 1, 0] = term(k, y_prev, 0).astype(jnp.bfloat16)
        send(y2_send.at[k, 1, 0], y2_recv.at[k, 1, 0], 1, y2_sem.at[k, 1], down)
        terms[slot, 0] = term(k, y_next, 0)
        terms[slot, 1] = term(k, y_prev, 1)
        terms[slot, 2] = term(k, y, 1 - x_lo)
        terms[slot, 3] = term(k, y, x_lo)

    def stage_b(k):
        slot = lax.rem(k, slots)
        await_bytes(y1_recv.at[k, 0], y1_sem.at[k, 0])
        y2_send[k, 0, 0] = (terms[slot, 0] + y1_recv[k, 0].astype(jnp.float32)).astype(jnp.bfloat16)
        send(y2_send.at[k, 0, 0], y2_recv.at[k, 0, 0], 1, y2_sem.at[k, 0], up)
        await_bytes(y1_recv.at[k, 1], y1_sem.at[k, 1])
        y2_send[k, 1, 1] = (terms[slot, 1] + y1_recv[k, 1].astype(jnp.float32)).astype(jnp.bfloat16)
        send(y2_send.at[k, 1, 1], y2_recv.at[k, 1, 1], 1, y2_sem.at[k, 1], down)

    def stage_c(k):
        slot = lax.rem(k, slots)
        await_bytes(y2_recv.at[k, 0], y2_sem.at[k, 0])
        await_bytes(y2_recv.at[k, 1], y2_sem.at[k, 1])

        def total(which, at_x):
            return (
                terms[slot, which]
                + y2_recv[k, 0, at_x].astype(jnp.float32)
                + y2_recv[k, 1, at_x].astype(jnp.float32)
            )

        x_send[k] = total(2, 1 - x_lo).astype(jnp.bfloat16)
        send(x_send.at[k], x_recv.at[k], 2, x_sem.at[k], beside)
        terms[slot, 3] = total(3, x_lo)

    def pack(k, arrays):
        for q in range(QUAD):
            for a in range(3):
                q1_send[k, q, a] = arrays[a][:, q * part : (q + 1) * part]
        for q in quads:
            send(q1_send.at[k, q], q1_recv.at[k, mine], 3, q1_sem.at[k], on_member(level, q))
        q1_recv[k, mine] = q1_send[k, mine]

    def spread(k):
        await_bytes(q1_recv.at[k, pl.ds(0, QUAD - 1)], q1_sem.at[k])
        q1_held[...] = q1_recv[k]
        for j in range(win_slots):
            chosen = q1_held[table[level * QUAD + j]]
            for z in range(LEVELS):
                z1_send[k, z, j] = chosen[:, z * 16 : (z + 1) * 16, :]
        for z in levels:
            send(z1_send.at[k, z], z1_recv.at[k, level], 4, z1_sem.at[k], on_member(z, mine))
        z1_recv[k, level] = z1_send[k, level]

    def stage_p(k):
        @pl.when(k == plain)
        def _():
            await_bytes(weight, load_sem.at[row_parts + 1])
            await_bytes(first, load_sem.at[row_parts + 2])
            await_bytes(second, load_sem.at[row_parts + 3])

        row, col = place(k)
        here = (pl.ds(row, ROWS), pl.ds(col, cols))
        pack(k, (weight[here].astype(jnp.bfloat16), first[here], second[here]))

    def stage_d(k):
        slot = lax.rem(k, slots)
        row, col = place(k)
        here = (pl.ds(row, ROWS), pl.ds(col, cols))
        await_bytes(x_recv.at[k], x_sem.at[k])
        gradient = terms[slot, 3] + x_recv[k].astype(jnp.float32)
        updated, moment_one, moment_two = adam(
            weight[here],
            first[here].astype(jnp.float32),
            second[here].astype(jnp.float32),
            gradient,
            jnp.full((1, cols), rates[member], jnp.float32),
            jnp.full((1, cols), decays_one[member], jnp.float32),
            jnp.full((1, cols), decays_two[member], jnp.float32),
        )
        out_weight[here] = updated
        out_first[here] = moment_one.astype(jnp.bfloat16)
        out_second[here] = moment_two.astype(jnp.bfloat16)

        @pl.when(k < plain)
        def _():
            pack(k, (out_weight[here].astype(jnp.bfloat16), out_first[here], out_second[here]))

        @pl.when(k >= plain)
        def _():
            e = k - plain
            for q in range(QUAD):
                g1_send[e, q] = gradient[:, q * part : (q + 1) * part].astype(jnp.bfloat16)
            for q in quads:
                send(g1_send.at[e, q], g1_recv.at[e, mine], 7, g1_sem.at[e], on_member(level, q))
            g1_recv[e, mine] = g1_send[e, mine]

    def stage_e(k):
        @pl.when(k < plain)
        def _():
            spread(k)

        @pl.when(k >= plain)
        def _():
            e = k - plain
            await_bytes(g1_recv.at[e, pl.ds(0, QUAD - 1)], g1_sem.at[e])
            g1_held[...] = g1_recv[e]
            for j in range(win_slots):
                chosen = g1_held[table[level * QUAD + j]]
                for z in range(LEVELS):
                    g2_send[e, z, j] = chosen[z * 16 : (z + 1) * 16, :]
            for z in levels:
                send(g2_send.at[e, z], g2_recv.at[e, level], 8, g2_sem.at[e], on_member(z, mine))
            g2_recv[e, level] = g2_send[e, level]

    def stage_f(k):
        await_bytes(z1_recv.at[k, pl.ds(0, LEVELS - 1)], z1_sem.at[k])
        z1_held[...] = z1_recv[k]

        @pl.when(k >= plain)
        def _():
            e = k - plain
            await_bytes(g2_recv.at[e, pl.ds(0, LEVELS - 1)], g2_sem.at[e])

            def step_level(z, carry):
                for j in range(win_slots):
                    who = z * QUAD + table[z * QUAD + j]
                    stepped = adam(
                        z1_held[z, j, 0].astype(jnp.float32),
                        z1_held[z, j, 1].astype(jnp.float32),
                        z1_held[z, j, 2].astype(jnp.float32),
                        g2_recv[e, z, j].astype(jnp.float32),
                        jnp.full((1, part), rates[who], jnp.float32),
                        jnp.full((1, part), decays_one[who], jnp.float32),
                        jnp.full((1, part), decays_two[who], jnp.float32),
                    )
                    for a in range(3):
                        z1_held[z, j, a] = stepped[a].astype(jnp.bfloat16)
                return carry

            lax.fori_loop(0, LEVELS, step_level, 0)

        for z in range(LEVELS):
            for j in range(lose_slots):
                source = table[32 + z * QUAD + j]
                z2_send[k, z, j] = z1_held[source // QUAD, lax.rem(source, QUAD)]
        for z in levels:
            send(z2_send.at[k, z], z2_recv.at[k, level], 5, z2_sem.at[k], on_member(z, mine))
        z2_recv[k, level] = z2_send[k, level]

    def stage_g(k):
        await_bytes(z2_recv.at[k, pl.ds(0, LEVELS - 1)], z2_sem.at[k])
        z2_held[...] = z2_recv[k]
        for q in range(QUAD):
            slot = table[64 + level * QUAD + q]
            for z in range(LEVELS):
                q2_send[k, q, z] = z2_held[z, slot]
        for q in quads:
            send(q2_send.at[k, q], q2_recv.at[k, mine], 6, q2_sem.at[k], on_member(level, q))
        q2_recv[k, mine] = q2_send[k, mine]

    outs = ((out_weight, weight_out), (out_first, first_out), (out_second, second_out))

    def stage_h(k):
        row, col = place(k)
        await_bytes(q2_recv.at[k, pl.ds(0, QUAD - 1)], q2_sem.at[k])
        taken = jnp.full((1, part), table[96 + member], jnp.int32) != 0
        for q in range(QUAD):
            for a in range(3):
                ref = outs[a][0]
                here = (pl.ds(row, ROWS), pl.ds(col + q * part, part))
                copied = q2_recv[k, q, :, a].reshape(ROWS, part).astype(jnp.float32)
                kept = ref[here].astype(jnp.float32)
                ref[here] = jnp.where(taken, copied, kept).astype(ref.dtype)
        for a in range(3):
            here = (pl.ds(row, ROWS), pl.ds(col, cols))
            pltpu.make_async_copy(outs[a][0].at[here], outs[a][1].at[here], out_sem.at[a]).start()

    stages = dict(
        a=stage_a,
        b=stage_b,
        c=stage_c,
        d=stage_d,
        e=stage_e,
        f=stage_f,
        g=stage_g,
        h=stage_h,
        p=stage_p,
        r=spread,
    )

    def iteration(i, carry):
        for name in order:
            lowest = plain if name in "pr" else 0
            k = i - lags[name] + lowest

            @pl.when((k >= lowest) & (k < chunks))
            def _():
                stages[name](k)

        return carry

    lax.fori_loop(0, chunks + lags["h"], iteration, 0)

    sent = (
        y1_send,
        y2_send,
        x_send,
        q1_send.at[:, pl.ds(0, QUAD - 1)],
        z1_send.at[:, pl.ds(0, LEVELS - 1)],
        z2_send.at[:, pl.ds(0, LEVELS - 1)],
        q2_send.at[:, pl.ds(0, QUAD - 1)],
        g1_send.at[:, pl.ds(0, QUAD - 1)],
        g2_send.at[:, pl.ds(0, LEVELS - 1)],
    )
    for stage, ref in enumerate(sent):
        await_bytes(ref, send_sem.at[stage])
    for a in range(3):
        await_bytes(outs[a][0], out_sem.at[a])


def step_call(plan, table, rates, ones, twos, *blocks):
    win_slots, lose_slots, order, lags = PLANS[plan]
    tokens, cotangent, weight, first, second = blocks
    rows, width = weight.shape
    cols = width // SPLIT
    chunks = rows // ROWS * SPLIT
    part = cols // QUAD
    kind = jnp.bfloat16
    scalars = pl.BlockSpec(memory_space=pltpu.SMEM)
    anywhere = pl.BlockSpec(memory_space=pl.ANY)
    like = [pltpu.VMEM(block.shape, block.dtype) for block in blocks]
    y1 = pltpu.VMEM((chunks, 2, ROWS, cols), kind)
    y2 = pltpu.VMEM((chunks, 2, 2, ROWS, cols), kind)
    beside = pltpu.VMEM((chunks, ROWS, cols), kind)
    q1 = pltpu.VMEM((chunks, QUAD, 3, ROWS, part), kind)
    z1 = pltpu.VMEM((chunks, LEVELS, win_slots, 3, ROWS // LEVELS, part), kind)
    z2 = pltpu.VMEM((chunks, LEVELS, lose_slots, 3, ROWS // LEVELS, part), kind)
    q2 = pltpu.VMEM((chunks, QUAD, LEVELS, 3, ROWS // LEVELS, part), kind)
    g1 = pltpu.VMEM((EARLY, QUAD, ROWS, part), kind)
    g2 = pltpu.VMEM((EARLY, LEVELS, win_slots, ROWS // LEVELS, part), kind)
    dma = pltpu.SemaphoreType.DMA
    return pl.pallas_call(
        functools.partial(step_kernel, win_slots, lose_slots, order, lags),
        out_shape=(
            jax.ShapeDtypeStruct(weight.shape, jnp.float32),
            jax.ShapeDtypeStruct(weight.shape, kind),
            jax.ShapeDtypeStruct(weight.shape, kind),
        ),
        in_specs=[scalars] * 4 + [anywhere] * 5,
        out_specs=(anywhere,) * 3,
        scratch_shapes=like
        + [like[2], like[3], like[4]]
        + [y1, y1, y2, y2, beside, beside, q1, q1, z1, z1, z2, z2, q2, q2, g1, g1, g2, g2]
        + [
            pltpu.VMEM((lags["d"] + 1, 4, ROWS, cols), jnp.float32),
            pltpu.VMEM(q1.shape[1:], kind),
            pltpu.VMEM(z1.shape[1:], kind),
            pltpu.VMEM(z2.shape[1:], kind),
            pltpu.VMEM(g1.shape[1:], kind),
            dma((rows // ROWS + 4,)),
            dma((3,)),
            dma((9,)),
            dma((chunks, 2)),
            dma((chunks, 2)),
            dma((chunks,)),
            dma((chunks,)),
            dma((chunks,)),
            dma((chunks,)),
            dma((chunks,)),
            dma((EARLY,)),
            dma((EARLY,)),
        ],
        compiler_params=pltpu.CompilerParams(
            collective_id=plan,
            has_side_effects=True,
            vmem_limit_bytes=63 * 2**20,
        ),
    )(table, rates, ones, twos, *blocks)


def route_kernel(sources, rates, perturb, table, plan, log_rate, winner, place):
    members = sources.shape[0]

    def clear(m, carry):
        winner[m] = 0
        for part in range(4):
            table[part * members + m] = 0
        return carry

    lax.fori_loop(0, members, clear, 0)

    def mark(m, carry):
        @pl.when(sources[m] != m)
        def _():
            winner[sources[m]] = 1

        return carry

    lax.fori_loop(0, members, mark, 0)

    def rank(z, most):
        wins = losses = jnp.int32(0)
        for q in range(QUAD):
            m = z * QUAD + q
            won = winner[m]
            lost = (sources[m] != m).astype(jnp.int32)
            place[m] = z * QUAD + wins
            table[2 * members + m] = jnp.where(lost != 0, losses, 0)
            table[3 * members + m] = lost

            @pl.when(won != 0)
            def _():
                table[z * QUAD + wins] = q

            wins += won
            losses += lost
        return jnp.maximum(most[0], wins), jnp.maximum(most[1], losses)

    wins, losses = lax.fori_loop(0, members // QUAD, rank, (jnp.int32(0), jnp.int32(0)))
    plan[0] = jnp.where(
        wins > 3, 3, jnp.where(losses > 3, 3, jnp.where(wins > 2, 2, jnp.where(losses > 2, 1, 0)))
    )

    def want(m, carry):
        @pl.when(sources[m] != m)
        def _():
            slot = (m // QUAD) * QUAD + table[2 * members + m]
            table[members + slot] = place[sources[m]]

        return carry

    lax.fori_loop(0, members, want, 0)
    lane = lax.broadcasted_iota(jnp.int32, log_rate.shape, 1)

    def gather(m, carry):
        rate, shift = carry
        source = sources[m]
        moved = jnp.where(source != m, perturb[m] - 1, 0)
        here = lane == m
        return jnp.where(here, rates[source], rate), jnp.where(here, moved, shift)

    start = (jnp.ones(log_rate.shape, jnp.float32), jnp.zeros(log_rate.shape, jnp.int32))
    rate, shift = lax.fori_loop(0, members, gather, start)
    log_rate[...] = jnp.log(rate) + shift.astype(jnp.float32) * math.log(2.0)


def route_call(sources, rates, perturb):
    members = sources.shape[0]
    scalars = pl.BlockSpec(memory_space=pltpu.SMEM)
    return pl.pallas_call(
        route_kernel,
        out_shape=(
            jax.ShapeDtypeStruct((4 * members,), jnp.int32),
            jax.ShapeDtypeStruct((1,), jnp.int32),
            jax.ShapeDtypeStruct((1, members), jnp.float32),
        ),
        in_specs=[scalars] * 3,
        out_specs=(scalars, scalars, pl.BlockSpec(memory_space=pltpu.VMEM)),
        scratch_shapes=[pltpu.SMEM((members,), jnp.int32)] * 2,
    )(sources, rates, perturb)


def copy_kernel(arrays, *refs):
    sources, targets, held = (refs[i * arrays : (i + 1) * arrays] for i in range(3))
    read_sem, write_sem = refs[3 * arrays :]
    pieces = read_sem.shape[1]
    reads, writes = [], []
    for p in range(pieces):
        for a in range(arrays):
            rows = sources[a].shape[0] // pieces
            here = pl.ds(p * rows, rows)
            reads.append(
                pltpu.make_async_copy(sources[a].at[here], held[a].at[here], read_sem.at[a, p])
            )
            writes.append(
                pltpu.make_async_copy(held[a].at[here], targets[a].at[here], write_sem.at[a, p])
            )
    for read in reads:
        read.start()
    for read, write in zip(reads, writes):
        read.wait()
        write.start()
    for write in writes:
        write.wait()


def copy_call(*arrays):
    anywhere = pl.BlockSpec(memory_space=pl.ANY)
    pieces = pltpu.SemaphoreType.DMA((len(arrays), 4))
    return pl.pallas_call(
        functools.partial(copy_kernel, len(arrays)),
        out_shape=tuple(jax.ShapeDtypeStruct(a.shape, a.dtype) for a in arrays),
        in_specs=[anywhere] * len(arrays),
        out_specs=(anywhere,) * len(arrays),
        scratch_shapes=[pltpu.VMEM(a.shape, a.dtype) for a in arrays] + [pieces, pieces],
        compiler_params=pltpu.CompilerParams(vmem_limit_bytes=32 * 2**20),
    )(*arrays)


def on_device(
    tokens,
    cotangent,
    weight,
    first_moment,
    second_moment,
    learn_rate,
    beta_one,
    beta_two,
    sources,
    perturb,
):
    table, plan, log_rate = route_call(sources, learn_rate, perturb)
    stepped = lax.switch(
        plan[0],
        [functools.partial(step_call, which) for which in range(len(PLANS))],
        table,
        learn_rate,
        beta_one,
        beta_two,
        tokens[0],
        cotangent[0],
        weight[0],
        first_moment[0],
        second_moment[0],
    )
    new_weight, new_first, new_second = copy_call(*stepped)
    return new_weight[None], new_first[None], new_second[None], log_rate[0]


def solution(mesh):
    block = P("member", "shard", None)
    return jax.shard_map(
        on_device,
        mesh=mesh,
        in_specs=(block,) * 5 + (P(),) * 5,
        out_specs=(block, block, block, P()),
        check_vma=False,
    )
```

```python
import functools
import math

import jax
import jax.numpy as jnp
from jax import lax
from jax.experimental import pallas as pl
from jax.experimental.pallas import tpu as pltpu
from jax.sharding import PartitionSpec as P

MESH = pl.DeviceIdType.MESH
ROWS = 128
SPLIT = 2
LEVELS = 8
QUAD = 4
RING = 4
PLANS = (
    (2, 2, True, 3, "sgfjtchdpibrea", dict(a=0, b=1, c=2, d=3, i=3, e=4, f=6, g=8, h=10, p=0, j=1, r=1, s=3, t=4)),
    (2, 2, False, 3, "ftsrcpdbaegh", dict(a=0, b=1, c=2, d=3, e=4, f=6, g=8, h=11, p=0, r=2, s=3, t=4)),
    (2, 3, False, 3, "efpdrctghsba", dict(a=0, b=1, c=2, d=3, e=4, f=6, g=8, h=11, p=0, r=1, s=2, t=5)),
    (3, 3, False, 2, "esdctprbhgaf", dict(a=0, b=1, c=2, d=3, e=4, f=5, g=7, h=10, p=0, r=1, s=3, t=5)),
    (4, 4, False, 1, "fdphtscbearg", dict(a=0, b=1, c=2, d=3, e=3, f=5, g=7, h=9, p=0, r=0, s=3, t=7)),
)


def twentieth_power(value):
    square = value * value
    fourth = square * square
    eighth = fourth * fourth
    return eighth * eighth * fourth


def adam(master, first, second, gradient, rate, decay_one, decay_two):
    scale_one = 1.0 / (1.0 - twentieth_power(decay_one))
    scale_two = 1.0 / (1.0 - twentieth_power(decay_two))
    moment_one = decay_one * first + (1.0 - decay_one) * gradient
    moment_two = decay_two * second + (1.0 - decay_two) * gradient * gradient
    updated = master - rate * (
        (moment_one * scale_one) / (jnp.sqrt(moment_two * scale_two) + 1e-08) + 0.1 * master
    )
    return updated, moment_one, moment_two


def step_kernel(
    plan,
    table,
    rates,
    decays_one,
    decays_two,
    tokens_in,
    cotangent_in,
    weight_in,
    first_in,
    second_in,
    weight_out,
    first_out,
    second_out,
    tokens,
    cotangent,
    weight,
    first,
    second,
    out_weight,
    out_first,
    out_second,
    y1_send,
    y1_recv,
    y2_send,
    y2_recv,
    x_send,
    x_recv,
    q1_send,
    q1_recv,
    z1_send,
    z1_recv,
    z2_send,
    z2_recv,
    q2_send,
    q2_recv,
    g1_send,
    g1_recv,
    g2_send,
    g2_recv,
    g3_send,
    g3_recv,
    g4_send,
    g4_recv,
    c1_recv,
    c2_recv,
    x1_send,
    x2_send,
    terms,
    q1_held,
    z1_held,
    z2_held,
    g1_held,
    g2_held,
    g3_held,
    load_sem,
    out_sem,
    send_sem,
    y1_sem,
    y2_sem,
    x_sem,
    q1_sem,
    z1_sem,
    z2_sem,
    q2_sem,
    g1_sem,
    g2_sem,
    g3_sem,
    g4_sem,
    c1_sem,
    c2_sem,
):
    win_slots, lose_slots, by_chip, early, order, lags = plan
    chunks = y1_send.shape[0]
    cols = y1_send.shape[3]
    plain = chunks - early
    part = cols // QUAD
    own_rows = weight.shape[0]
    slots = terms.shape[0]
    member = lax.axis_index("member")
    shard = lax.axis_index("shard")
    level, mine = member // QUAD, lax.rem(member, QUAD)
    y, x_lo = shard // 2, lax.rem(shard, 2)
    y_next, y_prev = lax.rem(y + 1, RING), lax.rem(y + RING - 1, RING)
    y_far = lax.rem(y + 2, RING)

    def on_shard(at_y, at_x):
        return {"member": member, "shard": at_y * 2 + at_x}

    def on_member(at_level, at_quad):
        return {"member": at_level * QUAD + at_quad, "shard": shard}

    up, down = on_shard(y_next, x_lo), on_shard(y_prev, x_lo)
    beside = on_shard(y, 1 - x_lo)
    column, core = mine // 2, lax.rem(mine, 2)
    quads = [lax.rem(mine + d, QUAD) for d in range(1, QUAD)]
    levels = [lax.rem(level + d, LEVELS) for d in (4, 3, 5, 2, 6, 1, 7)]

    row_parts = own_rows // ROWS
    blocks = tokens.shape[1] // own_rows

    def load(src, dst, which):
        pltpu.make_async_copy(src, dst, load_sem.at[which]).start()

    def load_tokens(part_of_rows):
        for b in range(blocks):
            here = pl.ds(b * own_rows + part_of_rows * ROWS, ROWS)
            load(tokens_in.at[:, here], tokens.at[:, here], part_of_rows)

    load(cotangent_in, cotangent, row_parts)
    load_tokens(0)
    load(weight_in, weight, row_parts + 1)
    load(first_in, first, row_parts + 2)
    load(second_in, second, row_parts + 3)
    for r in range(1, row_parts):
        load_tokens(r)

    peers = [up, down, beside]
    peers += [on_member(level, q) for q in quads]
    peers += [on_member(z, mine) for z in levels]
    barrier = pltpu.get_barrier_semaphore()
    for peer in peers:
        pl.semaphore_signal(barrier, inc=1, device_id=peer, device_id_type=MESH)
    pl.semaphore_wait(barrier, len(peers))

    def send(src, dst, stage, recv, device):
        pltpu.make_async_remote_copy(
            src_ref=src,
            dst_ref=dst,
            send_sem=send_sem.at[stage],
            recv_sem=recv,
            device_id=device,
            device_id_type=MESH,
        ).start()

    def await_bytes(ref, sem):
        pltpu.make_async_copy(ref, ref, sem).wait()

    def place(k):
        row = pl.multiple_of((k // SPLIT) * ROWS, ROWS)
        col = pl.multiple_of(lax.rem(k, SPLIT) * cols, cols)
        return row, col

    def term(k, at_y, at_x):
        row, col = place(k)
        start = pl.multiple_of((at_y * 2 + at_x) * own_rows + row, ROWS)
        return lax.dot_general(
            tokens[:, pl.ds(start, ROWS)],
            cotangent[:, pl.ds(col, cols)],
            (((0,), (0,)), ((), ())),
            preferred_element_type=jnp.float32,
        )

    def stage_a(k):
        slot = lax.rem(k, slots)

        @pl.when(k == 0)
        def _():
            await_bytes(cotangent, load_sem.at[row_parts])

        @pl.when(lax.rem(k, SPLIT) == 0)
        def _():
            await_bytes(tokens.at[:, pl.ds(0, blocks * ROWS)], load_sem.at[k // SPLIT])

        y1_send[k, 0] = term(k, y_far, 0).astype(jnp.bfloat16)
        send(y1_send.at[k, 0], y1_recv.at[k, 0], 0, y1_sem.at[k, 0], up)
        y1_send[k, 1] = term(k, y_far, 1).astype(jnp.bfloat16)
        send(y1_send.at[k, 1], y1_recv.at[k, 1], 0, y1_sem.at[k, 1], down)
        y2_send[k, 0, 1] = term(k, y_next, 1).astype(jnp.bfloat16)
        send(y2_send.at[k, 0, 1], y2_recv.at[k, 0, 1], 1, y2_sem.at[k, 0], up)
        y2_send[k, 1, 0] = term(k, y_prev, 0).astype(jnp.bfloat16)
        send(y2_send.at[k, 1, 0], y2_recv.at[k, 1, 0], 1, y2_sem.at[k, 1], down)
        terms[slot, 0] = term(k, y_next, 0)
        terms[slot, 1] = term(k, y_prev, 1)
        terms[slot, 2] = term(k, y, 1 - x_lo)
        terms[slot, 3] = term(k, y, x_lo)

    def stage_b(k):
        slot = lax.rem(k, slots)
        await_bytes(y1_recv.at[k, 0], y1_sem.at[k, 0])
        y2_send[k, 0, 0] = (terms[slot, 0] + y1_recv[k, 0].astype(jnp.float32)).astype(jnp.bfloat16)
        send(y2_send.at[k, 0, 0], y2_recv.at[k, 0, 0], 1, y2_sem.at[k, 0], up)
        await_bytes(y1_recv.at[k, 1], y1_sem.at[k, 1])
        y2_send[k, 1, 1] = (terms[slot, 1] + y1_recv[k, 1].astype(jnp.float32)).astype(jnp.bfloat16)
        send(y2_send.at[k, 1, 1], y2_recv.at[k, 1, 1], 1, y2_sem.at[k, 1], down)

    def stage_c(k):
        slot = lax.rem(k, slots)
        await_bytes(y2_recv.at[k, 0], y2_sem.at[k, 0])
        await_bytes(y2_recv.at[k, 1], y2_sem.at[k, 1])

        def total(which, at_x):
            return (
                terms[slot, which]
                + y2_recv[k, 0, at_x].astype(jnp.float32)
                + y2_recv[k, 1, at_x].astype(jnp.float32)
            )

        x_send[k] = total(2, 1 - x_lo).astype(jnp.bfloat16)
        send(x_send.at[k], x_recv.at[k], 2, x_sem.at[k], beside)
        terms[slot, 3] = total(3, x_lo)

    def split(block, blocks, sem, chip_blocks, chip_sem, stage):
        if by_chip:
            for x in range(2):
                q = x * 2 + 1 - core
                there = on_member(level, column * 2 + 1 - core)
                send(block.at[q], chip_blocks.at[x], stage, chip_sem, there)
        else:
            for q in quads:
                send(block.at[q], blocks.at[mine], stage, sem, on_member(level, q))
            blocks[mine] = block[mine]

    def cross(block, chip_blocks, chip_sem, crossing, blocks, sem, held, stage):
        await_bytes(chip_blocks, chip_sem)
        for x in range(2):
            held[x] = block[x * 2 + core]
            held[2 + x] = chip_blocks[x]
        other = (table[level * QUAD + column] + core) % 2
        for x in range(2):
            crossing[x] = held[other * 2 + x]
        blocks[column] = crossing[column]
        there = on_member(level, (1 - column) * 2 + core)
        send(crossing.at[1 - column], blocks.at[column], stage, sem, there)

    def select(blocks, sem, held, out, stage, targets, target_sem):
        if by_chip:
            await_bytes(blocks.at[pl.ds(0, 1)], sem)
        else:
            await_bytes(blocks.at[pl.ds(0, QUAD - 1)], sem)
            held[...] = blocks[...]
        for j in range(win_slots):
            chosen = blocks[j] if by_chip else held[table[level * QUAD + j]]
            for z in range(LEVELS):
                out[z, j] = chosen[..., z * 16 : (z + 1) * 16, :]
        for z in levels:
            send(out.at[z], targets.at[level], stage, target_sem, on_member(z, mine))
        targets[level] = out[level]

    def forward(blocks, sem, held, out, stage, targets, target_sem):
        await_bytes(blocks.at[pl.ds(0, LEVELS - 1)], sem)
        held[...] = blocks[...]
        for z in range(LEVELS):
            for j in range(lose_slots):
                source = table[32 + z * QUAD + j]
                out[z, j] = held[source // QUAD, lax.rem(source, QUAD)]
        for z in levels:
            send(out.at[z], targets.at[level], stage, target_sem, on_member(z, mine))
        targets[level] = out[level]

    def deliver(blocks, sem, held, out, stage, targets, target_sem):
        await_bytes(blocks.at[pl.ds(0, LEVELS - 1)], sem)
        held[...] = blocks[...]
        for q in range(QUAD):
            slot = table[64 + level * QUAD + q]
            for z in range(LEVELS):
                out[q, z] = held[z, slot]
        for q in quads:
            send(out.at[q], targets.at[mine], stage, target_sem, on_member(level, q))
        targets[mine] = out[mine]

    def pack(k, arrays):
        for q in range(QUAD):
            for a in range(3):
                q1_send[k, q, a] = arrays[a][:, q * part : (q + 1) * part]
        split(q1_send.at[k], q1_recv.at[k], q1_sem.at[k], c1_recv.at[k], c1_sem.at[k], 3)

    def cross_state(k):
        cross(
            q1_send.at[k],
            c1_recv.at[k],
            c1_sem.at[k],
            x1_send.at[k],
            q1_recv.at[k],
            q1_sem.at[k],
            q1_held,
            10,
        )

    def select_state(k):
        select(q1_recv.at[k], q1_sem.at[k], q1_held, z1_send.at[k], 4, z1_recv.at[k], z1_sem.at[k])

    def forward_state(k):
        forward(z1_recv.at[k], z1_sem.at[k], z1_held, z2_send.at[k], 5, z2_recv.at[k], z2_sem.at[k])

    def deliver_state(k):
        deliver(z2_recv.at[k], z2_sem.at[k], z2_held, q2_send.at[k], 6, q2_recv.at[k], q2_sem.at[k])

    def cross_gradient(e):
        cross(
            g1_send.at[e],
            c2_recv.at[e],
            c2_sem.at[e],
            x2_send.at[e],
            g1_recv.at[e],
            g1_sem.at[e],
            g1_held,
            11,
        )

    def select_gradient(e):
        select(g1_recv.at[e], g1_sem.at[e], g1_held, g2_send.at[e], 7, g2_recv.at[e], g2_sem.at[e])

    def forward_gradient(e):
        forward(g2_recv.at[e], g2_sem.at[e], g2_held, g3_send.at[e], 8, g3_recv.at[e], g3_sem.at[e])

    def deliver_gradient(e):
        deliver(g3_recv.at[e], g3_sem.at[e], g3_held, g4_send.at[e], 9, g4_recv.at[e], g4_sem.at[e])

    def either(k, state, gradient):
        @pl.when(k < plain)
        def _():
            state(k)

        @pl.when(k >= plain)
        def _():
            gradient(k - plain)

    def stage_p(k):
        @pl.when(k == plain)
        def _():
            await_bytes(weight, load_sem.at[row_parts + 1])
            await_bytes(first, load_sem.at[row_parts + 2])
            await_bytes(second, load_sem.at[row_parts + 3])

        row, col = place(k)
        here = (pl.ds(row, ROWS), pl.ds(col, cols))
        pack(k, (weight[here].astype(jnp.bfloat16), first[here], second[here]))

    def stage_d(k):
        slot = lax.rem(k, slots)
        row, col = place(k)
        here = (pl.ds(row, ROWS), pl.ds(col, cols))
        await_bytes(x_recv.at[k], x_sem.at[k])
        gradient = terms[slot, 3] + x_recv[k].astype(jnp.float32)
        updated, moment_one, moment_two = adam(
            weight[here],
            first[here].astype(jnp.float32),
            second[here].astype(jnp.float32),
            gradient,
            jnp.full((1, cols), rates[member], jnp.float32),
            jnp.full((1, cols), decays_one[member], jnp.float32),
            jnp.full((1, cols), decays_two[member], jnp.float32),
        )
        out_weight[here] = updated
        out_first[here] = moment_one.astype(jnp.bfloat16)
        out_second[here] = moment_two.astype(jnp.bfloat16)

        @pl.when(k < plain)
        def _():
            pack(k, (out_weight[here].astype(jnp.bfloat16), out_first[here], out_second[here]))

        @pl.when(k >= plain)
        def _():
            e = k - plain
            for q in range(QUAD):
                g1_send[e, q] = gradient[:, q * part : (q + 1) * part].astype(jnp.bfloat16)
            split(g1_send.at[e], g1_recv.at[e], g1_sem.at[e], c2_recv.at[e], c2_sem.at[e], 12)

    def stage_i(k):
        either(k, cross_state, cross_gradient)

    def stage_e(k):
        either(k, select_state, select_gradient)

    def stage_f(k):
        either(k, forward_state, forward_gradient)

    def stage_g(k):
        either(k, deliver_state, deliver_gradient)

    outs = ((out_weight, weight_out), (out_first, first_out), (out_second, second_out))

    def stage_h(k):
        row, col = place(k)
        await_bytes(q2_recv.at[k, pl.ds(0, QUAD - 1)], q2_sem.at[k])
        source = table[96 + member]
        taken = jnp.full((1, part), source, jnp.int32) != member

        def keep_or_take(q, copied):
            here = (pl.ds(row, ROWS), pl.ds(col + q * part, part))
            for a in range(3):
                ref = outs[a][0]
                kept = ref[here].astype(jnp.float32)
                ref[here] = jnp.where(taken, copied[a], kept).astype(ref.dtype)

        def arrived(q):
            return [q2_recv[k, q, :, a].reshape(ROWS, part).astype(jnp.float32) for a in range(3)]

        @pl.when(k < plain)
        def _():
            for q in range(QUAD):
                keep_or_take(q, arrived(q))

        @pl.when(k >= plain)
        def _():
            e = k - plain
            await_bytes(g4_recv.at[e, pl.ds(0, QUAD - 1)], g4_sem.at[e])
            hyper = [jnp.full((1, part), ref[source]) for ref in (rates, decays_one, decays_two)]
            for q in range(QUAD):
                gradient = g4_recv[e, q].reshape(ROWS, part).astype(jnp.float32)
                keep_or_take(q, adam(*arrived(q), gradient, *hyper))

        for a in range(3):
            here = (pl.ds(row, ROWS), pl.ds(col, cols))
            pltpu.make_async_copy(outs[a][0].at[here], outs[a][1].at[here], out_sem.at[a]).start()

    stages = dict(
        a=stage_a,
        b=stage_b,
        c=stage_c,
        d=stage_d,
        e=stage_e,
        f=stage_f,
        g=stage_g,
        h=stage_h,
        i=stage_i,
        p=stage_p,
        j=cross_state,
        r=select_state,
        s=forward_state,
        t=deliver_state,
    )

    def iteration(i, carry):
        for name in order:
            lowest = plain if name in "pjrst" else 0
            k = i - lags[name] + lowest

            @pl.when((k >= lowest) & (k < chunks))
            def _():
                stages[name](k)

        return carry

    lax.fori_loop(0, chunks + lags["h"], iteration, 0)

    others, peers = pl.ds(0, 2 if by_chip else QUAD - 1), pl.ds(0, QUAD - 1)
    away = pl.ds(0, LEVELS - 1)
    sent = [
        (0, y1_send),
        (1, y2_send),
        (2, x_send),
        (3, q1_send.at[:, others]),
        (12, g1_send.at[:, others]),
        (4, z1_send.at[:, away]),
        (5, z2_send.at[:, away]),
        (6, q2_send.at[:, peers]),
        (7, g2_send.at[:, away]),
        (8, g3_send.at[:, away]),
        (9, g4_send.at[:, peers]),
    ]
    if by_chip:
        sent += [(10, x1_send.at[:, pl.ds(0, 1)]), (11, x2_send.at[:, pl.ds(0, 1)])]
    for stage, ref in sent:
        await_bytes(ref, send_sem.at[stage])
    for a in range(3):
        await_bytes(outs[a][0], out_sem.at[a])


def step_call(plan, table, rates, ones, twos, *blocks):
    win_slots, lose_slots, by_chip, early, order, lags = PLANS[plan]
    tokens, cotangent, weight, first, second = blocks
    rows, width = weight.shape
    cols = width // SPLIT
    chunks = rows // ROWS * SPLIT
    part = cols // QUAD
    kind = jnp.bfloat16
    scalars = pl.BlockSpec(memory_space=pltpu.SMEM)
    anywhere = pl.BlockSpec(memory_space=pl.ANY)
    like = [pltpu.VMEM(block.shape, block.dtype) for block in blocks]
    y1 = pltpu.VMEM((chunks, 2, ROWS, cols), kind)
    y2 = pltpu.VMEM((chunks, 2, 2, ROWS, cols), kind)
    beside = pltpu.VMEM((chunks, ROWS, cols), kind)
    q1 = pltpu.VMEM((chunks, QUAD, 3, ROWS, part), kind)
    z1 = pltpu.VMEM((chunks, LEVELS, win_slots, 3, ROWS // LEVELS, part), kind)
    z2 = pltpu.VMEM((chunks, LEVELS, lose_slots, 3, ROWS // LEVELS, part), kind)
    q2 = pltpu.VMEM((chunks, QUAD, LEVELS, 3, ROWS // LEVELS, part), kind)
    g1 = pltpu.VMEM((early, QUAD, ROWS, part), kind)
    g2 = pltpu.VMEM((early, LEVELS, win_slots, ROWS // LEVELS, part), kind)
    g3 = pltpu.VMEM((early, LEVELS, lose_slots, ROWS // LEVELS, part), kind)
    g4 = pltpu.VMEM((early, QUAD, LEVELS, ROWS // LEVELS, part), kind)
    chip = (chunks, early) if by_chip else (1, 1)
    c1 = pltpu.VMEM((chip[0], 2, 3, ROWS, part), kind)
    c2 = pltpu.VMEM((chip[1], 2, ROWS, part), kind)
    dma = pltpu.SemaphoreType.DMA
    return pl.pallas_call(
        functools.partial(step_kernel, PLANS[plan]),
        out_shape=(
            jax.ShapeDtypeStruct(weight.shape, jnp.float32),
            jax.ShapeDtypeStruct(weight.shape, kind),
            jax.ShapeDtypeStruct(weight.shape, kind),
        ),
        in_specs=[scalars] * 4 + [anywhere] * 5,
        out_specs=(anywhere,) * 3,
        scratch_shapes=like
        + [like[2], like[3], like[4]]
        + [y1, y1, y2, y2, beside, beside, q1, q1, z1, z1, z2, z2, q2, q2]
        + [g1, g1, g2, g2, g3, g3, g4, g4, c1, c2, c1, c2]
        + [
            pltpu.VMEM((lags["d"] + 1, 4, ROWS, cols), jnp.float32),
            pltpu.VMEM(q1.shape[1:], kind),
            pltpu.VMEM(z1.shape[1:], kind),
            pltpu.VMEM(z2.shape[1:], kind),
            pltpu.VMEM(g1.shape[1:], kind),
            pltpu.VMEM(g2.shape[1:], kind),
            pltpu.VMEM(g3.shape[1:], kind),
            dma((rows // ROWS + 4,)),
            dma((3,)),
            dma((13,)),
            dma((chunks, 2)),
            dma((chunks, 2)),
            dma((chunks,)),
            dma((chunks,)),
            dma((chunks,)),
            dma((chunks,)),
            dma((chunks,)),
            dma((early,)),
            dma((early,)),
            dma((early,)),
            dma((early,)),
            dma((chunks,)),
            dma((early,)),
        ],
        compiler_params=pltpu.CompilerParams(
            collective_id=plan,
            has_side_effects=True,
            vmem_limit_bytes=63 * 2**20,
        ),
    )(table, rates, ones, twos, *blocks)


def route_kernel(sources, rates, perturb, table, plan, log_rate, winner, place):
    members = sources.shape[0]

    def clear(m, carry):
        winner[m] = 0
        for part in range(4):
            table[part * members + m] = 0
        return carry

    lax.fori_loop(0, members, clear, 0)

    def mark(m, carry):
        @pl.when(sources[m] != m)
        def _():
            winner[sources[m]] = 1

        return carry

    lax.fori_loop(0, members, mark, 0)

    def count(z, most):
        wins = losses = pair = jnp.int32(0)
        for q in range(QUAD):
            m = z * QUAD + q
            lost = sources[m] != m
            table[2 * members + m] = jnp.where(lost, losses, 0)
            table[3 * members + m] = sources[m]
            wins += winner[m]
            losses += lost.astype(jnp.int32)
            if q % 2:
                pair = jnp.maximum(pair, winner[m - 1] + winner[m])
        return tuple(jnp.maximum(a, b) for a, b in zip(most, (wins, losses, pair)))

    nothing = (jnp.int32(0),) * 3
    wins, losses, pair = lax.fori_loop(0, members // QUAD, count, nothing)
    chosen = jnp.int32(len(PLANS) - 1)
    for p in reversed(range(len(PLANS))):
        fits = (wins <= PLANS[p][0]) & (losses <= PLANS[p][1])
        if PLANS[p][2]:
            fits &= pair <= 1
        chosen = jnp.where(fits, p, chosen)
    plan[0] = chosen
    by_chip = jnp.bool_(False)
    for p in range(len(PLANS)):
        if PLANS[p][2]:
            by_chip |= chosen == p

    def rank(z, carry):
        wins = jnp.int32(0)
        for q in range(QUAD):
            m = z * QUAD + q
            slot = z * QUAD + jnp.where(by_chip, q // 2, wins)
            place[m] = slot

            @pl.when(winner[m] != 0)
            def _():
                table[slot] = jnp.where(by_chip, q % 2, q)

            wins += winner[m]
        return carry

    lax.fori_loop(0, members // QUAD, rank, 0)

    def want(m, carry):
        @pl.when(sources[m] != m)
        def _():
            slot = (m // QUAD) * QUAD + table[2 * members + m]
            table[members + slot] = place[sources[m]]

        return carry

    lax.fori_loop(0, members, want, 0)
    lane = lax.broadcasted_iota(jnp.int32, log_rate.shape, 1)

    def gather(m, carry):
        rate, shift = carry
        source = sources[m]
        moved = jnp.where(source != m, perturb[m] - 1, 0)
        here = lane == m
        return jnp.where(here, rates[source], rate), jnp.where(here, moved, shift)

    start = (jnp.ones(log_rate.shape, jnp.float32), jnp.zeros(log_rate.shape, jnp.int32))
    rate, shift = lax.fori_loop(0, members, gather, start)
    log_rate[...] = jnp.log(rate) + shift.astype(jnp.float32) * math.log(2.0)


def route_call(sources, rates, perturb):
    members = sources.shape[0]
    scalars = pl.BlockSpec(memory_space=pltpu.SMEM)
    return pl.pallas_call(
        route_kernel,
        out_shape=(
            jax.ShapeDtypeStruct((4 * members,), jnp.int32),
            jax.ShapeDtypeStruct((1,), jnp.int32),
            jax.ShapeDtypeStruct((1, members), jnp.float32),
        ),
        in_specs=[scalars] * 3,
        out_specs=(scalars, scalars, pl.BlockSpec(memory_space=pltpu.VMEM)),
        scratch_shapes=[pltpu.SMEM((members,), jnp.int32)] * 2,
    )(sources, rates, perturb)


def copy_kernel(arrays, *refs):
    sources, targets, held = (refs[i * arrays : (i + 1) * arrays] for i in range(3))
    read_sem, write_sem = refs[3 * arrays :]
    pieces = read_sem.shape[1]
    reads, writes = [], []
    for p in range(pieces):
        for a in range(arrays):
            rows = sources[a].shape[0] // pieces
            here = pl.ds(p * rows, rows)
            reads.append(
                pltpu.make_async_copy(sources[a].at[here], held[a].at[here], read_sem.at[a, p])
            )
            writes.append(
                pltpu.make_async_copy(held[a].at[here], targets[a].at[here], write_sem.at[a, p])
            )
    for read in reads:
        read.start()
    for read, write in zip(reads, writes):
        read.wait()
        write.start()
    for write in writes:
        write.wait()


def copy_call(*arrays):
    anywhere = pl.BlockSpec(memory_space=pl.ANY)
    pieces = pltpu.SemaphoreType.DMA((len(arrays), 4))
    return pl.pallas_call(
        functools.partial(copy_kernel, len(arrays)),
        out_shape=tuple(jax.ShapeDtypeStruct(a.shape, a.dtype) for a in arrays),
        in_specs=[anywhere] * len(arrays),
        out_specs=(anywhere,) * len(arrays),
        scratch_shapes=[pltpu.VMEM(a.shape, a.dtype) for a in arrays] + [pieces, pieces],
        compiler_params=pltpu.CompilerParams(vmem_limit_bytes=32 * 2**20),
    )(*arrays)


def on_device(
    tokens,
    cotangent,
    weight,
    first_moment,
    second_moment,
    learn_rate,
    beta_one,
    beta_two,
    sources,
    perturb,
):
    table, plan, log_rate = route_call(sources, learn_rate, perturb)
    stepped = lax.switch(
        plan[0],
        [functools.partial(step_call, which) for which in range(len(PLANS))],
        table,
        learn_rate,
        beta_one,
        beta_two,
        tokens[0],
        cotangent[0],
        weight[0],
        first_moment[0],
        second_moment[0],
    )
    new_weight, new_first, new_second = copy_call(*stepped)
    return new_weight[None], new_first[None], new_second[None], log_rate[0]


def solution(mesh):
    block = P("member", "shard", None)
    return jax.shard_map(
        on_device,
        mesh=mesh,
        in_specs=(block,) * 5 + (P(),) * 5,
        out_specs=(block, block, block, P()),
        check_vma=False,
    )
```

```python
import functools
import math

import jax
import jax.numpy as jnp
from jax import lax
from jax.experimental import pallas as pl
from jax.experimental.pallas import tpu as pltpu
from jax.sharding import PartitionSpec as P

MESH = pl.DeviceIdType.MESH
ROWS = 128
SPLIT = 2
LEVELS = 8
QUAD = 4
RING = 4
PLANS = (
    (2, 2, True, 3, "sgfjtchdpibrea", dict(a=0, b=1, c=2, d=3, i=3, e=4, f=6, g=8, h=10, p=0, j=1, r=1, s=3, t=4)),
    (2, 2, False, 3, "ftsrcpdbaegh", dict(a=0, b=1, c=2, d=3, e=4, f=6, g=8, h=11, p=0, r=2, s=3, t=4)),
    (2, 3, False, 3, "efpdrctghsba", dict(a=0, b=1, c=2, d=3, e=4, f=6, g=8, h=11, p=0, r=1, s=2, t=5)),
    (3, 3, False, 2, "esdctprbhgaf", dict(a=0, b=1, c=2, d=3, e=4, f=5, g=7, h=10, p=0, r=1, s=3, t=5)),
    (4, 4, False, 1, "fdphtscbearg", dict(a=0, b=1, c=2, d=3, e=3, f=5, g=7, h=9, p=0, r=0, s=3, t=7)),
)


def twentieth_power(value):
    square = value * value
    fourth = square * square
    eighth = fourth * fourth
    return eighth * eighth * fourth


def adam(master, first, second, gradient, rate, decay_one, decay_two):
    scale_one = 1.0 / (1.0 - twentieth_power(decay_one))
    scale_two = 1.0 / (1.0 - twentieth_power(decay_two))
    moment_one = decay_one * first + (1.0 - decay_one) * gradient
    moment_two = decay_two * second + (1.0 - decay_two) * gradient * gradient
    updated = master - rate * (
        (moment_one * scale_one) / (jnp.sqrt(moment_two * scale_two) + 1e-08) + 0.1 * master
    )
    return updated, moment_one, moment_two


def step_kernel(
    plan,
    table,
    rates,
    decays_one,
    decays_two,
    tokens_in,
    cotangent_in,
    weight_in,
    first_in,
    second_in,
    weight_out,
    first_out,
    second_out,
    tokens,
    cotangent,
    weight,
    first,
    second,
    out_weight,
    out_first,
    out_second,
    y1_send,
    y1_recv,
    y2_send,
    y2_recv,
    x_send,
    x_recv,
    q1_send,
    q1_recv,
    z1_send,
    z1_recv,
    z2_send,
    z2_recv,
    q2_send,
    q2_recv,
    g1_send,
    g1_recv,
    g2_send,
    g2_recv,
    g3_send,
    g3_recv,
    g4_send,
    g4_recv,
    c1_recv,
    c2_recv,
    x1_send,
    x2_send,
    terms,
    q1_held,
    z1_held,
    z2_held,
    g1_held,
    g2_held,
    g3_held,
    load_sem,
    out_sem,
    send_sem,
    y1_sem,
    y2_sem,
    x_sem,
    q1_sem,
    z1_sem,
    z2_sem,
    q2_sem,
    g1_sem,
    g2_sem,
    g3_sem,
    g4_sem,
    c1_sem,
    c2_sem,
):
    win_slots, lose_slots, by_chip, early, order, lags = plan
    chunks = y1_send.shape[0]
    cols = y1_send.shape[3]
    plain = chunks - early
    part = cols // QUAD
    own_rows = weight.shape[0]
    slots = terms.shape[0]
    member = lax.axis_index("member")
    shard = lax.axis_index("shard")
    level, mine = member // QUAD, lax.rem(member, QUAD)
    y, x_lo = shard // 2, lax.rem(shard, 2)
    y_next, y_prev = lax.rem(y + 1, RING), lax.rem(y + RING - 1, RING)
    y_far = lax.rem(y + 2, RING)

    def on_shard(at_y, at_x):
        return {"member": member, "shard": at_y * 2 + at_x}

    def on_member(at_level, at_quad):
        return {"member": at_level * QUAD + at_quad, "shard": shard}

    up, down = on_shard(y_next, x_lo), on_shard(y_prev, x_lo)
    beside = on_shard(y, 1 - x_lo)
    column, core = mine // 2, lax.rem(mine, 2)
    quads = [lax.rem(mine + d, QUAD) for d in range(1, QUAD)]
    levels = [lax.rem(level + d, LEVELS) for d in (4, 3, 5, 2, 6, 1, 7)]

    row_parts = own_rows // ROWS
    blocks = tokens.shape[1] // own_rows

    def load(src, dst, which):
        pltpu.make_async_copy(src, dst, load_sem.at[which]).start()

    def load_tokens(part_of_rows):
        for b in range(blocks):
            here = pl.ds(b * own_rows + part_of_rows * ROWS, ROWS)
            load(tokens_in.at[:, here], tokens.at[:, here], part_of_rows)

    load(cotangent_in, cotangent, row_parts)
    load_tokens(0)
    load(weight_in, weight, row_parts + 1)
    load(first_in, first, row_parts + 2)
    load(second_in, second, row_parts + 3)
    for r in range(1, row_parts):
        load_tokens(r)

    peers = [up, down, beside]
    peers += [on_member(level, q) for q in quads]
    peers += [on_member(z, mine) for z in levels]
    barrier = pltpu.get_barrier_semaphore()
    for peer in peers:
        pl.semaphore_signal(barrier, inc=1, device_id=peer, device_id_type=MESH)
    pl.semaphore_wait(barrier, len(peers))

    def send(src, dst, stage, recv, device):
        pltpu.make_async_remote_copy(
            src_ref=src,
            dst_ref=dst,
            send_sem=send_sem.at[stage],
            recv_sem=recv,
            device_id=device,
            device_id_type=MESH,
        ).start()

    def await_bytes(ref, sem):
        pltpu.make_async_copy(ref, ref, sem).wait()

    def place(k):
        row = pl.multiple_of((k // SPLIT) * ROWS, ROWS)
        col = pl.multiple_of(lax.rem(k, SPLIT) * cols, cols)
        return row, col

    def term(k, at_y, at_x):
        row, col = place(k)
        start = pl.multiple_of((at_y * 2 + at_x) * own_rows + row, ROWS)
        return lax.dot_general(
            tokens[:, pl.ds(start, ROWS)],
            cotangent[:, pl.ds(col, cols)],
            (((0,), (0,)), ((), ())),
            preferred_element_type=jnp.float32,
        )

    def stage_a(k):
        slot = lax.rem(k, slots)

        @pl.when(k == 0)
        def _():
            await_bytes(cotangent, load_sem.at[row_parts])

        @pl.when(lax.rem(k, SPLIT) == 0)
        def _():
            await_bytes(tokens.at[:, pl.ds(0, blocks * ROWS)], load_sem.at[k // SPLIT])

        y1_send[k, 0] = term(k, y_far, 0).astype(jnp.bfloat16)
        send(y1_send.at[k, 0], y1_recv.at[k, 0], 0, y1_sem.at[k, 0], up)
        y1_send[k, 1] = term(k, y_far, 1).astype(jnp.bfloat16)
        send(y1_send.at[k, 1], y1_recv.at[k, 1], 0, y1_sem.at[k, 1], down)
        y2_send[k, 0, 1] = term(k, y_next, 1).astype(jnp.bfloat16)
        send(y2_send.at[k, 0, 1], y2_recv.at[k, 0, 1], 1, y2_sem.at[k, 0], up)
        y2_send[k, 1, 0] = term(k, y_prev, 0).astype(jnp.bfloat16)
        send(y2_send.at[k, 1, 0], y2_recv.at[k, 1, 0], 1, y2_sem.at[k, 1], down)
        terms[slot, 0] = term(k, y_next, 0)
        terms[slot, 1] = term(k, y_prev, 1)
        terms[slot, 2] = term(k, y, 1 - x_lo)
        terms[slot, 3] = term(k, y, x_lo)

    def stage_b(k):
        slot = lax.rem(k, slots)
        await_bytes(y1_recv.at[k, 0], y1_sem.at[k, 0])
        y2_send[k, 0, 0] = (terms[slot, 0] + y1_recv[k, 0].astype(jnp.float32)).astype(jnp.bfloat16)
        send(y2_send.at[k, 0, 0], y2_recv.at[k, 0, 0], 1, y2_sem.at[k, 0], up)
        await_bytes(y1_recv.at[k, 1], y1_sem.at[k, 1])
        y2_send[k, 1, 1] = (terms[slot, 1] + y1_recv[k, 1].astype(jnp.float32)).astype(jnp.bfloat16)
        send(y2_send.at[k, 1, 1], y2_recv.at[k, 1, 1], 1, y2_sem.at[k, 1], down)

    def stage_c(k):
        slot = lax.rem(k, slots)
        await_bytes(y2_recv.at[k, 0], y2_sem.at[k, 0])
        await_bytes(y2_recv.at[k, 1], y2_sem.at[k, 1])

        def total(which, at_x):
            return (
                terms[slot, which]
                + y2_recv[k, 0, at_x].astype(jnp.float32)
                + y2_recv[k, 1, at_x].astype(jnp.float32)
            )

        x_send[k] = total(2, 1 - x_lo).astype(jnp.bfloat16)
        send(x_send.at[k], x_recv.at[k], 2, x_sem.at[k], beside)
        terms[slot, 3] = total(3, x_lo)

    def split(block, blocks, sem, chip_blocks, chip_sem, stage):
        if by_chip:
            for x in range(2):
                q = x * 2 + 1 - core
                there = on_member(level, column * 2 + 1 - core)
                send(block.at[q], chip_blocks.at[x], stage, chip_sem, there)
        else:
            for q in quads:
                send(block.at[q], blocks.at[mine], stage, sem, on_member(level, q))
            blocks[mine] = block[mine]

    def cross(block, chip_blocks, chip_sem, crossing, blocks, sem, held, stage):
        await_bytes(chip_blocks, chip_sem)
        for x in range(2):
            held[x] = block[x * 2 + core]
            held[2 + x] = chip_blocks[x]
        other = (table[level * QUAD + column] + core) % 2
        for x in range(2):
            crossing[x] = held[other * 2 + x]
        blocks[column] = crossing[column]
        there = on_member(level, (1 - column) * 2 + core)
        send(crossing.at[1 - column], blocks.at[column], stage, sem, there)

    def select(blocks, sem, held, out, stage, targets, target_sem):
        if by_chip:
            await_bytes(blocks.at[pl.ds(0, 1)], sem)
        else:
            await_bytes(blocks.at[pl.ds(0, QUAD - 1)], sem)
            held[...] = blocks[...]
        for j in range(win_slots):
            chosen = blocks[j] if by_chip else held[table[level * QUAD + j]]
            for z in range(LEVELS):
                out[z, j] = chosen[..., z * 16 : (z + 1) * 16, :]
        for z in levels:
            send(out.at[z], targets.at[level], stage, target_sem, on_member(z, mine))
        targets[level] = out[level]

    def forward(blocks, sem, held, out, stage, targets, target_sem):
        await_bytes(blocks.at[pl.ds(0, LEVELS - 1)], sem)
        held[...] = blocks[...]
        for z in range(LEVELS):
            for j in range(lose_slots):
                source = table[32 + z * QUAD + j]
                out[z, j] = held[source // QUAD, lax.rem(source, QUAD)]
        for z in levels:
            send(out.at[z], targets.at[level], stage, target_sem, on_member(z, mine))
        targets[level] = out[level]

    def deliver(blocks, sem, held, out, stage, targets, target_sem):
        await_bytes(blocks.at[pl.ds(0, LEVELS - 1)], sem)
        held[...] = blocks[...]
        for q in range(QUAD):
            slot = table[64 + level * QUAD + q]
            for z in range(LEVELS):
                out[q, z] = held[z, slot]
        for q in quads:
            send(out.at[q], targets.at[mine], stage, target_sem, on_member(level, q))
        targets[mine] = out[mine]

    def pack(k, arrays):
        for q in range(QUAD):
            for a in range(3):
                q1_send[k, q, a] = arrays[a][:, q * part : (q + 1) * part]
        split(q1_send.at[k], q1_recv.at[k], q1_sem.at[k], c1_recv.at[k], c1_sem.at[k], 3)

    def cross_state(k):
        cross(
            q1_send.at[k],
            c1_recv.at[k],
            c1_sem.at[k],
            x1_send.at[k],
            q1_recv.at[k],
            q1_sem.at[k],
            q1_held,
            10,
        )

    def select_state(k):
        select(q1_recv.at[k], q1_sem.at[k], q1_held, z1_send.at[k], 4, z1_recv.at[k], z1_sem.at[k])

    def forward_state(k):
        forward(z1_recv.at[k], z1_sem.at[k], z1_held, z2_send.at[k], 5, z2_recv.at[k], z2_sem.at[k])

    def deliver_state(k):
        deliver(z2_recv.at[k], z2_sem.at[k], z2_held, q2_send.at[k], 6, q2_recv.at[k], q2_sem.at[k])

    def cross_gradient(e):
        cross(
            g1_send.at[e],
            c2_recv.at[e],
            c2_sem.at[e],
            x2_send.at[e],
            g1_recv.at[e],
            g1_sem.at[e],
            g1_held,
            11,
        )

    def select_gradient(e):
        select(g1_recv.at[e], g1_sem.at[e], g1_held, g2_send.at[e], 7, g2_recv.at[e], g2_sem.at[e])

    def forward_gradient(e):
        forward(g2_recv.at[e], g2_sem.at[e], g2_held, g3_send.at[e], 8, g3_recv.at[e], g3_sem.at[e])

    def deliver_gradient(e):
        deliver(g3_recv.at[e], g3_sem.at[e], g3_held, g4_send.at[e], 9, g4_recv.at[e], g4_sem.at[e])

    def either(k, state, gradient):
        @pl.when(k < plain)
        def _():
            state(k)

        @pl.when(k >= plain)
        def _():
            gradient(k - plain)

    def stage_p(k):
        @pl.when(k == plain)
        def _():
            await_bytes(weight, load_sem.at[row_parts + 1])
            await_bytes(first, load_sem.at[row_parts + 2])
            await_bytes(second, load_sem.at[row_parts + 3])

        row, col = place(k)
        here = (pl.ds(row, ROWS), pl.ds(col, cols))
        pack(k, (weight[here].astype(jnp.bfloat16), first[here], second[here]))

    def stage_d(k):
        slot = lax.rem(k, slots)
        row, col = place(k)
        here = (pl.ds(row, ROWS), pl.ds(col, cols))
        await_bytes(x_recv.at[k], x_sem.at[k])
        gradient = terms[slot, 3] + x_recv[k].astype(jnp.float32)
        updated, moment_one, moment_two = adam(
            weight[here],
            first[here].astype(jnp.float32),
            second[here].astype(jnp.float32),
            gradient,
            jnp.full((1, cols), rates[member], jnp.float32),
            jnp.full((1, cols), decays_one[member], jnp.float32),
            jnp.full((1, cols), decays_two[member], jnp.float32),
        )
        out_weight[here] = updated
        out_first[here] = moment_one.astype(jnp.bfloat16)
        out_second[here] = moment_two.astype(jnp.bfloat16)

        @pl.when(k < plain)
        def _():
            pack(k, (out_weight[here].astype(jnp.bfloat16), out_first[here], out_second[here]))

        @pl.when(k >= plain)
        def _():
            e = k - plain
            for q in range(QUAD):
                g1_send[e, q] = gradient[:, q * part : (q + 1) * part].astype(jnp.bfloat16)
            split(g1_send.at[e], g1_recv.at[e], g1_sem.at[e], c2_recv.at[e], c2_sem.at[e], 12)

    def stage_i(k):
        either(k, cross_state, cross_gradient)

    def stage_e(k):
        either(k, select_state, select_gradient)

    def stage_f(k):
        either(k, forward_state, forward_gradient)

    def stage_g(k):
        either(k, deliver_state, deliver_gradient)

    outs = ((out_weight, weight_out), (out_first, first_out), (out_second, second_out))

    def stage_h(k):
        row, col = place(k)
        await_bytes(q2_recv.at[k, pl.ds(0, QUAD - 1)], q2_sem.at[k])
        source = table[96 + member]
        taken = jnp.full((1, part), source, jnp.int32) != member

        def keep_or_take(q, copied):
            here = (pl.ds(row, ROWS), pl.ds(col + q * part, part))
            for a in range(3):
                ref = outs[a][0]
                kept = ref[here].astype(jnp.float32)
                ref[here] = jnp.where(taken, copied[a], kept).astype(ref.dtype)

        def arrived(q):
            return [q2_recv[k, q, :, a].reshape(ROWS, part).astype(jnp.float32) for a in range(3)]

        @pl.when(k < plain)
        def _():
            for q in range(QUAD):
                keep_or_take(q, arrived(q))

        @pl.when(k >= plain)
        def _():
            e = k - plain
            await_bytes(g4_recv.at[e, pl.ds(0, QUAD - 1)], g4_sem.at[e])
            hyper = [jnp.full((1, part), ref[source]) for ref in (rates, decays_one, decays_two)]
            for q in range(QUAD):
                gradient = g4_recv[e, q].reshape(ROWS, part).astype(jnp.float32)
                keep_or_take(q, adam(*arrived(q), gradient, *hyper))

        for a in range(3):
            here = (pl.ds(row, ROWS), pl.ds(col, cols))
            pltpu.make_async_copy(outs[a][0].at[here], outs[a][1].at[here], out_sem.at[a]).start()

    stages = dict(
        a=stage_a,
        b=stage_b,
        c=stage_c,
        d=stage_d,
        e=stage_e,
        f=stage_f,
        g=stage_g,
        h=stage_h,
        i=stage_i,
        p=stage_p,
        j=cross_state,
        r=select_state,
        s=forward_state,
        t=deliver_state,
    )

    def iteration(i, carry):
        for name in order:
            lowest = plain if name in "pjrst" else 0
            k = i - lags[name] + lowest

            @pl.when((k >= lowest) & (k < chunks))
            def _():
                stages[name](k)

        return carry

    lax.fori_loop(0, chunks + lags["h"], iteration, 0)

    others, peers = pl.ds(0, 2 if by_chip else QUAD - 1), pl.ds(0, QUAD - 1)
    away = pl.ds(0, LEVELS - 1)
    sent = [
        (0, y1_send),
        (1, y2_send),
        (2, x_send),
        (3, q1_send.at[:, others]),
        (12, g1_send.at[:, others]),
        (4, z1_send.at[:, away]),
        (5, z2_send.at[:, away]),
        (6, q2_send.at[:, peers]),
        (7, g2_send.at[:, away]),
        (8, g3_send.at[:, away]),
        (9, g4_send.at[:, peers]),
    ]
    if by_chip:
        sent += [(10, x1_send.at[:, pl.ds(0, 1)]), (11, x2_send.at[:, pl.ds(0, 1)])]
    for stage, ref in sent:
        await_bytes(ref, send_sem.at[stage])
    for a in range(3):
        await_bytes(outs[a][0], out_sem.at[a])


def step_call(plan, table, rates, ones, twos, *blocks):
    win_slots, lose_slots, by_chip, early, order, lags = PLANS[plan]
    tokens, cotangent, weight, first, second = blocks
    rows, width = weight.shape
    cols = width // SPLIT
    chunks = rows // ROWS * SPLIT
    part = cols // QUAD
    kind = jnp.bfloat16
    scalars = pl.BlockSpec(memory_space=pltpu.SMEM)
    anywhere = pl.BlockSpec(memory_space=pl.ANY)
    like = [pltpu.VMEM(block.shape, block.dtype) for block in blocks]
    y1 = pltpu.VMEM((chunks, 2, ROWS, cols), kind)
    y2 = pltpu.VMEM((chunks, 2, 2, ROWS, cols), kind)
    beside = pltpu.VMEM((chunks, ROWS, cols), kind)
    q1 = pltpu.VMEM((chunks, QUAD, 3, ROWS, part), kind)
    z1 = pltpu.VMEM((chunks, LEVELS, win_slots, 3, ROWS // LEVELS, part), kind)
    z2 = pltpu.VMEM((chunks, LEVELS, lose_slots, 3, ROWS // LEVELS, part), kind)
    q2 = pltpu.VMEM((chunks, QUAD, LEVELS, 3, ROWS // LEVELS, part), kind)
    g1 = pltpu.VMEM((early, QUAD, ROWS, part), kind)
    g2 = pltpu.VMEM((early, LEVELS, win_slots, ROWS // LEVELS, part), kind)
    g3 = pltpu.VMEM((early, LEVELS, lose_slots, ROWS // LEVELS, part), kind)
    g4 = pltpu.VMEM((early, QUAD, LEVELS, ROWS // LEVELS, part), kind)
    chip = (chunks, early) if by_chip else (1, 1)
    c1 = pltpu.VMEM((chip[0], 2, 3, ROWS, part), kind)
    c2 = pltpu.VMEM((chip[1], 2, ROWS, part), kind)
    dma = pltpu.SemaphoreType.DMA
    return pl.pallas_call(
        functools.partial(step_kernel, PLANS[plan]),
        out_shape=(
            jax.ShapeDtypeStruct(weight.shape, jnp.float32),
            jax.ShapeDtypeStruct(weight.shape, kind),
            jax.ShapeDtypeStruct(weight.shape, kind),
        ),
        in_specs=[scalars] * 4 + [anywhere] * 5,
        out_specs=(anywhere,) * 3,
        scratch_shapes=like
        + [like[2], like[3], like[4]]
        + [y1, y1, y2, y2, beside, beside, q1, q1, z1, z1, z2, z2, q2, q2]
        + [g1, g1, g2, g2, g3, g3, g4, g4, c1, c2, c1, c2]
        + [
            pltpu.VMEM((lags["d"] + 1, 4, ROWS, cols), jnp.float32),
            pltpu.VMEM(q1.shape[1:], kind),
            pltpu.VMEM(z1.shape[1:], kind),
            pltpu.VMEM(z2.shape[1:], kind),
            pltpu.VMEM(g1.shape[1:], kind),
            pltpu.VMEM(g2.shape[1:], kind),
            pltpu.VMEM(g3.shape[1:], kind),
            dma((rows // ROWS + 4,)),
            dma((3,)),
            dma((13,)),
            dma((chunks, 2)),
            dma((chunks, 2)),
            dma((chunks,)),
            dma((chunks,)),
            dma((chunks,)),
            dma((chunks,)),
            dma((chunks,)),
            dma((early,)),
            dma((early,)),
            dma((early,)),
            dma((early,)),
            dma((chunks,)),
            dma((early,)),
        ],
        compiler_params=pltpu.CompilerParams(
            collective_id=plan,
            has_side_effects=True,
            vmem_limit_bytes=63 * 2**20,
        ),
    )(table, rates, ones, twos, *blocks)


def route_kernel(sources, rates, perturb, table, plan, log_rate, winner, place):
    members = sources.shape[0]

    def clear(m, carry):
        winner[m] = 0
        for part in range(4):
            table[part * members + m] = 0
        return carry

    lax.fori_loop(0, members, clear, 0, unroll=True)

    def mark(m, carry):
        @pl.when(sources[m] != m)
        def _():
            winner[sources[m]] = 1

        return carry

    lax.fori_loop(0, members, mark, 0, unroll=True)

    def count(z, most):
        wins = losses = pair = jnp.int32(0)
        for q in range(QUAD):
            m = z * QUAD + q
            lost = sources[m] != m
            table[2 * members + m] = jnp.where(lost, losses, 0)
            table[3 * members + m] = sources[m]
            wins += winner[m]
            losses += lost.astype(jnp.int32)
            if q % 2:
                pair = jnp.maximum(pair, winner[m - 1] + winner[m])
        return tuple(jnp.maximum(a, b) for a, b in zip(most, (wins, losses, pair)))

    nothing = (jnp.int32(0),) * 3
    wins, losses, pair = lax.fori_loop(0, members // QUAD, count, nothing, unroll=True)
    chosen = jnp.int32(len(PLANS) - 1)
    for p in reversed(range(len(PLANS))):
        fits = (wins <= PLANS[p][0]) & (losses <= PLANS[p][1])
        if PLANS[p][2]:
            fits &= pair <= 1
        chosen = jnp.where(fits, p, chosen)
    plan[0] = chosen
    by_chip = jnp.bool_(False)
    for p in range(len(PLANS)):
        if PLANS[p][2]:
            by_chip |= chosen == p

    def rank(z, carry):
        wins = jnp.int32(0)
        for q in range(QUAD):
            m = z * QUAD + q
            slot = z * QUAD + jnp.where(by_chip, q // 2, wins)
            place[m] = slot

            @pl.when(winner[m] != 0)
            def _():
                table[slot] = jnp.where(by_chip, q % 2, q)

            wins += winner[m]
        return carry

    lax.fori_loop(0, members // QUAD, rank, 0, unroll=True)

    def want(m, carry):
        @pl.when(sources[m] != m)
        def _():
            slot = (m // QUAD) * QUAD + table[2 * members + m]
            table[members + slot] = place[sources[m]]

        return carry

    lax.fori_loop(0, members, want, 0, unroll=True)
    lane = lax.broadcasted_iota(jnp.int32, log_rate.shape, 1)

    def gather(m, carry):
        rate, shift = carry
        source = sources[m]
        moved = jnp.where(source != m, perturb[m] - 1, 0)
        here = lane == m
        return jnp.where(here, rates[source], rate), jnp.where(here, moved, shift)

    start = (jnp.ones(log_rate.shape, jnp.float32), jnp.zeros(log_rate.shape, jnp.int32))
    rate, shift = lax.fori_loop(0, members, gather, start, unroll=True)
    log_rate[...] = jnp.log(rate) + shift.astype(jnp.float32) * math.log(2.0)


def route_call(sources, rates, perturb):
    members = sources.shape[0]
    scalars = pl.BlockSpec(memory_space=pltpu.SMEM)
    return pl.pallas_call(
        route_kernel,
        out_shape=(
            jax.ShapeDtypeStruct((4 * members,), jnp.int32),
            jax.ShapeDtypeStruct((1,), jnp.int32),
            jax.ShapeDtypeStruct((1, members), jnp.float32),
        ),
        in_specs=[scalars] * 3,
        out_specs=(scalars, scalars, pl.BlockSpec(memory_space=pltpu.VMEM)),
        scratch_shapes=[pltpu.SMEM((members,), jnp.int32)] * 2,
    )(sources, rates, perturb)


def copy_kernel(arrays, *refs):
    sources, targets, held = (refs[i * arrays : (i + 1) * arrays] for i in range(3))
    read_sem, write_sem = refs[3 * arrays :]
    pieces = read_sem.shape[1]
    reads, writes = [], []
    for p in range(pieces):
        for a in range(arrays):
            rows = sources[a].shape[0] // pieces
            here = pl.ds(p * rows, rows)
            reads.append(
                pltpu.make_async_copy(sources[a].at[here], held[a].at[here], read_sem.at[a, p])
            )
            writes.append(
                pltpu.make_async_copy(held[a].at[here], targets[a].at[here], write_sem.at[a, p])
            )
    for read in reads:
        read.start()
    for read, write in zip(reads, writes):
        read.wait()
        write.start()
    for write in writes:
        write.wait()


def copy_call(*arrays):
    anywhere = pl.BlockSpec(memory_space=pl.ANY)
    pieces = pltpu.SemaphoreType.DMA((len(arrays), 4))
    return pl.pallas_call(
        functools.partial(copy_kernel, len(arrays)),
        out_shape=tuple(jax.ShapeDtypeStruct(a.shape, a.dtype) for a in arrays),
        in_specs=[anywhere] * len(arrays),
        out_specs=(anywhere,) * len(arrays),
        scratch_shapes=[pltpu.VMEM(a.shape, a.dtype) for a in arrays] + [pieces, pieces],
        compiler_params=pltpu.CompilerParams(vmem_limit_bytes=32 * 2**20),
    )(*arrays)


def on_device(
    tokens,
    cotangent,
    weight,
    first_moment,
    second_moment,
    learn_rate,
    beta_one,
    beta_two,
    sources,
    perturb,
):
    table, plan, log_rate = route_call(sources, learn_rate, perturb)
    stepped = lax.switch(
        plan[0],
        [functools.partial(step_call, which) for which in range(len(PLANS))],
        table,
        learn_rate,
        beta_one,
        beta_two,
        tokens[0],
        cotangent[0],
        weight[0],
        first_moment[0],
        second_moment[0],
    )
    new_weight, new_first, new_second = copy_call(*stepped)
    return new_weight[None], new_first[None], new_second[None], log_rate[0]


def solution(mesh):
    block = P("member", "shard", None)
    return jax.shard_map(
        on_device,
        mesh=mesh,
        in_specs=(block,) * 5 + (P(),) * 5,
        out_specs=(block, block, block, P()),
        check_vma=False,
    )
```
